32 devices in a mesh: grp: 4 (over y, x), rep: 8 (over z, core).
Axes of the slice: x: 2, y: 2, z: 4, core: 2. Of those that a mesh axis runs over, the one named last changes fastest.
Arguments:
- tokens: bfloat16 [8, 2048, 1024], P('rep', 'grp'), may hold values from -6 to 6
- cotangent: bfloat16 [8, 2048, 1024], P('rep', 'grp'), may hold values from -6 to 6
- order: int32 [8, 2048], P('rep'), may hold values from 0 to 2047, each once within a row
- lengths: int32 [8, 3], P('rep'), may hold values from 1 to 1024, 2048 in all within a row
- vectors: float32 [14688], replicated, may hold values from -7.6 to 1.5, as said below
- vector_moment: float32 [14688], replicated, may hold values from -6 to 6
- in_master: float32 [1024, 4384], P('grp'), may hold values from -0.1875 to 0.1875
- in_moment: float32 [1024, 4384], P('grp'), may hold values from -12 to 12
- in_error: float32 [8, 1024, 4384], P('rep', 'grp'), may hold values from -48 to 48
- in_factor: float32 [4384, 8], replicated, may hold values from -6 to 6
- out_master: float32 [2048, 1024], P('grp'), may hold values from -0.125 to 0.125
- out_moment: float32 [2048, 1024], P('grp'), may hold values from -12 to 12
- out_error: float32 [8, 2048, 1024], P('rep', 'grp'), may hold values from -48 to 48
- out_factor: float32 [1024, 8], replicated, may hold values from -6 to 6
Outputs:
- mixed: bfloat16 [8, 2048, 1024], P('rep', 'grp')
- input_grad: bfloat16 [8, 2048, 1024], P('rep', 'grp')
- in_grad: float32 [8, 1024, 4384], P('rep', 'grp')
- out_grad: float32 [8, 2048, 1024], P('rep', 'grp')
- vector_grad: float32 [14688], replicated
- in_new: float32 [1024, 4384], P('grp')
- in_moment_new: float32 [1024, 4384], P('grp')
- in_error_new: float32 [8, 1024, 4384], P('rep', 'grp')
- in_factor_new: float32 [4384, 8], replicated
- out_new: float32 [2048, 1024], P('grp')
- out_moment_new: float32 [2048, 1024], P('grp')
- out_error_new: float32 [8, 2048, 1024], P('rep', 'grp')
- out_factor_new: float32 [1024, 8], replicated
- vector_new: float32 [14688], replicated
- vector_moment_new: float32 [14688], replicated
The draws below stay inside these ranges and needn't reach their ends.
Inputs may be any that keep to these rules, and one draw needn't show every extreme that they name: Each row of order holds every number of 0 to 2047 once. Each row of lengths sums to 2048; its largest entry is exactly 1024. `vectors`: norm and gated-norm gains lie in 0.85 to 1.15, convolution weights in -0.9 to 0.9, convolution bias in -0.3 to 0.3, step bias in -3 to 0, decay logarithm in -7.6 to -1.2, skip gain in 0.5 to 1.5.
All inputs are finite; a program needn't handle non-finite values.
Results may differ from the reference program's by a relative error of at most 0.011.
Values may be sent and summed in bfloat16 or wider, within the bound.
A program may use at most 192 MiB of HBM per device.

```python
import math
from functools import partial
import jax
import jax.numpy as jnp
import numpy as np
from jax import lax

D = 1024
HEADS = 32
HEADDIM = 64
STATE = 128
CONV = 4
BLOCK = 256
RANK = 8
NSEQ = 3
INNER = 2048
XBC = 2304
IN_W = 4384
VEC = 14688
TOK_GRP = 2048
MAXLEN = 1024
N_REP = 8


def draw_vectors(key, part):
    subkeys = jax.random.split(key, 7)
    norm_gain = 1.0 + 0.15 * jax.random.uniform(subkeys[0], (D,), jnp.float32, -1.0, 1.0)
    conv_weight = jax.random.uniform(subkeys[1], (CONV * XBC,), jnp.float32, -0.9, 0.9)
    conv_bias = jax.random.uniform(subkeys[2], (XBC,), jnp.float32, -0.3, 0.3)
    dt_bias = jax.random.uniform(subkeys[3], (HEADS,), jnp.float32, -3.0, 0.0)
    decay_log = jax.random.uniform(subkeys[4], (HEADS,), jnp.float32, -7.6, -1.2)
    skip_gain = jax.random.uniform(subkeys[5], (HEADS,), jnp.float32, 0.5, 1.5)
    gate_gain = 1.0 + 0.15 * jax.random.uniform(subkeys[6], (INNER,), jnp.float32, -1.0, 1.0)
    return jnp.concatenate([norm_gain, conv_weight, conv_bias, dt_bias, decay_log, skip_gain, gate_gain])


def level_of(stream_key, extent, shards, low, top_value):
    def one(dim, shards_of):
        steps = jax.random.uniform(jax.random.fold_in(jax.random.fold_in(stream_key, 6), dim), (shards_of,), jnp.float32, low / len(shards), top_value / len(shards))
        return jnp.repeat(jnp.exp(steps), extent[dim] // shards_of).reshape((-1,) + (1,) * (len(extent) - dim - 1))

    loudness = one(*shards[0])
    for cut in shards[1:]:
        loudness = loudness * one(*cut)
    return loudness


def length_profile(count, total, most, skew):
    portions = [(1 << 20) // math.isqrt(standing ** skew) + 1 for standing in range(2, count + 1)]
    rest, given = total - most - (count - 1), [1] * (count - 1)
    while rest > 0:
        free = [i for i in range(count - 1) if given[i] < most]
        whole, budget = sum([portions[i] for i in free]), rest
        for i in free:
            extra = min(most - given[i], max(1, budget * portions[i] // whole), rest)
            given[i] = given[i] + extra
            rest = rest - extra
    return np.array([most] + given)


def uneven_parts(own_key, amount, total, most, skew):
    if amount == 2:
        one = jax.random.randint(own_key, (), max(1, total - most), min(most, total - 1) + 1)
        return jnp.stack([one, total - one])
    sizes = jnp.asarray(length_profile(amount, total, most, skew), jnp.int32)
    couples = (amount - 1) // 2
    donor, receiver = sizes[1:1 + 2 * couples:2], sizes[2:2 + 2 * couples:2]
    slack = jnp.minimum(donor - 1, most - receiver)
    shifted = jax.random.randint(jax.random.fold_in(own_key, 1), (couples,), 0, 1 << 20) % (slack + 1)
    sizes = sizes.at[1:1 + 2 * couples:2].set(donor - shifted).at[2:2 + 2 * couples:2].set(receiver + shifted)
    return sizes[jax.random.permutation(jax.random.fold_in(own_key, 2), amount)]


def bell_draw(own_key, dims, deviation, limit, shards=(), kind=jnp.bfloat16):
    drawn = deviation * jax.random.normal(own_key, dims, jnp.float32)
    if shards:
        drawn = drawn * level_of(own_key, dims, shards, -0.22, 0.18)
    return jnp.clip(drawn, -limit, limit).astype(kind)


def setup_inputs(seed: int = 0) -> dict:
    streams_of = jax.random.split(jax.random.key(seed), 15)
    return {
        "tokens": bell_draw(streams_of[0], (N_REP, TOK_GRP, D), 1.0, 6.0, ((0, 8), (1, 4))),
        "cotangent": bell_draw(streams_of[1], (N_REP, TOK_GRP, D), 1.0, 6.0, ((0, 8), (1, 4))),
        "order": jax.vmap(lambda own: jax.random.permutation(own, TOK_GRP))(jax.random.split(streams_of[2], N_REP)).reshape((N_REP, TOK_GRP)).astype(jnp.int32),
        "lengths": jax.vmap(lambda own: uneven_parts(own, NSEQ, TOK_GRP, MAXLEN, 2))(jax.random.split(streams_of[3], N_REP)).reshape((N_REP, NSEQ)).astype(jnp.int32),
        "vectors": draw_vectors(jax.random.fold_in(streams_of[14], 71), 0),
        "vector_moment": bell_draw(streams_of[5], (VEC,), 1.0, 6.0, (), jnp.float32),
        "in_master": bell_draw(streams_of[6], (D, IN_W), D ** -0.5, 0.1875, ((0, 4),), jnp.float32),
        "in_moment": bell_draw(streams_of[7], (D, IN_W), 2.0, 12.0, ((0, 4),), jnp.float32),
        "in_error": bell_draw(streams_of[8], (N_REP, D, IN_W), 8.0, 48.0, ((0, 8), (1, 4)), jnp.float32),
        "in_factor": bell_draw(streams_of[9], (IN_W, RANK), 1.0, 6.0, (), jnp.float32),
        "out_master": bell_draw(streams_of[10], (INNER, D), INNER ** -0.5, 0.125, ((0, 4),), jnp.float32),
        "out_moment": bell_draw(streams_of[11], (INNER, D), 2.0, 12.0, ((0, 4),), jnp.float32),
        "out_error": bell_draw(streams_of[12], (N_REP, INNER, D), 8.0, 48.0, ((0, 8), (1, 4)), jnp.float32),
        "out_factor": bell_draw(streams_of[13], (D, RANK), 1.0, 6.0, (), jnp.float32),
    }


epsilon = 1e-05
momentum_decay = 0.9
weight_rate = 0.001
vector_rate = 0.02
highest = lax.Precision.HIGHEST

@jax.custom_vjp
def low(v):
    return lax.optimization_barrier(v.astype(jnp.bfloat16)).astype(jnp.float32)

@jax.custom_vjp
def low_back(v):
    return v

def low_keep(v):
    return (low(v), None)

def low_pass(kept, grad):
    return (grad,)

def back_keep(v):
    return (v, None)

def back_low(kept, grad):
    return (low(grad),)
low.defvjp(low_keep, low_pass)
low_back.defvjp(back_keep, back_low)

def split_vectors(vectors):
    widths = [D, CONV * XBC, XBC, HEADS, HEADS, HEADS, INNER]
    pieces = []
    offset = 0
    for span_size in widths:
        pieces.append(vectors[offset:offset + span_size])
        offset = offset + span_size
    norm_gain, conv_flat, conv_bias, dt_bias, decay_log, skip_gain, gate_gain = pieces
    return (norm_gain, conv_flat.reshape(CONV, XBC), conv_bias, dt_bias, decay_log, skip_gain, gate_gain)

def rms_scale(values, gain):
    return values * lax.rsqrt(lax.optimization_barrier(jnp.mean(values * values, axis=-1, keepdims=True)) + epsilon) * gain

def gated_norm(mixer_out, gate_in, gain):
    return rms_scale(mixer_out * jax.nn.silu(gate_in), gain)

def causal_conv(padded, conv_weight, conv_bias, segment_pad):
    reach_rows = CONV - 1
    total_rows = padded.shape[0] - reach_rows
    accumulated = jnp.zeros((total_rows, padded.shape[1]), jnp.float32) + conv_bias[None, :]
    for tap_index in range(CONV):
        same_seq = (segment_pad[tap_index:tap_index + total_rows] == segment_pad[reach_rows:]).astype(jnp.float32)
        accumulated = accumulated + conv_weight[tap_index][None, :] * padded[tap_index:tap_index + total_rows] * same_seq[:, None]
    return jax.nn.silu(accumulated)

def prepare(mixed_in, dt_raw, dt_bias, decay_log):
    row_count = mixed_in.shape[0]
    head_values = mixed_in[:, :INNER].reshape(row_count, HEADS, HEADDIM)
    write_keys = mixed_in[:, INNER:INNER + STATE]
    read_keys = mixed_in[:, INNER + STATE:]
    step_sizes = jax.nn.softplus(dt_raw + dt_bias[None, :])
    log_decay = -jnp.exp(decay_log)[None, :] * step_sizes
    return (head_values, write_keys, read_keys, step_sizes, log_decay)

def block_step(skip_gain, state_in, pieces):
    head_values, write_keys, read_keys, step_sizes, log_decay, segment, before = pieces
    cum_decay = jnp.cumsum(log_decay, axis=0)
    block_len = segment.shape[0]
    index_row = jnp.arange(block_len)
    same_seq = (segment[:, None] == segment[None, :]) & (index_row[:, None] >= index_row[None, :])
    log_gap = jnp.where(same_seq[:, :, None], cum_decay[:, None, :] - cum_decay[None, :, :], -1e+30)
    read_write = jnp.dot(read_keys.astype(jnp.float32), write_keys.T.astype(jnp.float32), precision=highest, preferred_element_type=jnp.float32)
    decay_tile = jnp.exp(log_gap) * read_write[:, :, None]
    scaled_values = head_values * step_sizes[:, :, None]
    local_out = jnp.einsum('tsh,shp->thp', decay_tile, scaled_values, precision=highest)
    carry_in = jnp.exp(cum_decay) * (segment == before).astype(jnp.float32)[:, None]
    carried_out = carry_in[:, :, None] * jnp.einsum('tn,hpn->thp', read_keys, state_in, precision=highest)
    tail_decay = jnp.exp(cum_decay[-1][None, :] - cum_decay) * (segment == segment[-1]).astype(jnp.float32)[:, None]
    fresh_state = jnp.einsum('sh,shp,sn->hpn', tail_decay, scaled_values, write_keys, precision=highest)
    new_state = carry_in[-1][:, None, None] * state_in + fresh_state
    return (new_state, local_out + carried_out + skip_gain[None, :, None] * head_values)

def run_blocks(mixed_in, dt_raw, dt_bias, decay_log, skip_gain, segment, first_before):
    row_count = mixed_in.shape[0]
    blocks = row_count // BLOCK
    head_values, write_keys, read_keys, step_sizes, log_decay = prepare(mixed_in, dt_raw, dt_bias, decay_log)
    befores = jnp.concatenate([jnp.reshape(first_before, (1,)), segment.reshape(blocks, BLOCK)[:-1, -1]]).astype(jnp.int32)
    pieces = (head_values.reshape(blocks, BLOCK, HEADS, HEADDIM), write_keys.reshape(blocks, BLOCK, STATE), read_keys.reshape(blocks, BLOCK, STATE), step_sizes.reshape(blocks, BLOCK, HEADS), log_decay.reshape(blocks, BLOCK, HEADS), segment.reshape(blocks, BLOCK), befores)
    start_state = jnp.zeros((HEADS, HEADDIM, STATE), jnp.float32)
    final_state, outputs = lax.scan(jax.checkpoint(partial(block_step, skip_gain)), start_state, pieces)
    return (final_state, outputs.reshape(row_count, HEADS, HEADDIM), read_keys, log_decay)

def forward(vectors, in_master, out_master, stream, segment_pad):
    norm_gain, conv_weight, conv_bias, dt_bias, decay_log, skip_gain, gate_gain = split_vectors(vectors)
    in_weight = low(in_master)
    out_weight = low(out_master)
    normed = low(rms_scale(stream, norm_gain))
    projected = low(low_back(jnp.dot(normed.astype(jnp.float32), in_weight.astype(jnp.float32), precision=highest, preferred_element_type=jnp.float32)))
    gate_in = projected[:, :INNER]
    conv_in = projected[:, INNER:INNER + XBC]
    dt_raw = projected[:, INNER + XBC:]
    padded = jnp.concatenate([jnp.zeros((CONV - 1, XBC), jnp.float32), conv_in], axis=0)
    mixed_in = low(causal_conv(padded, conv_weight, conv_bias, segment_pad))
    final_state, outputs, read_keys, log_decay = run_blocks(mixed_in, dt_raw, dt_bias, decay_log, skip_gain, segment_pad[CONV - 1:], jnp.asarray(-1, jnp.int32))
    mixer_out = outputs.reshape(stream.shape[0], INNER)
    normed_out = low(gated_norm(mixer_out, gate_in, gate_gain))
    return stream + jnp.dot(normed_out.astype(jnp.float32), out_weight.astype(jnp.float32), precision=highest, preferred_element_type=jnp.float32)

def compress_update(grads, errors, factor, moment, master, replicas):
    merged = grads + errors
    left_factor = jnp.einsum('rij,jk->ik', merged, factor, precision=highest)
    gram_matrix = jnp.dot(left_factor.T.astype(jnp.float32), left_factor.astype(jnp.float32), precision=highest, preferred_element_type=jnp.float32)
    chol_factor = jnp.linalg.cholesky(gram_matrix)
    basis_rows = lax.linalg.triangular_solve(chol_factor, left_factor, left_side=False, lower=True, transpose_a=True)
    right_factor = jnp.einsum('rij,ik->jk', merged, basis_rows, precision=highest) / replicas
    approx = jnp.dot(basis_rows.astype(jnp.float32), right_factor.T.astype(jnp.float32), precision=highest, preferred_element_type=jnp.float32)
    errors_new = merged - approx[None]
    moment_new = momentum_decay * moment + approx
    master_new = master - weight_rate * moment_new
    return (master_new, moment_new, errors_new, right_factor)

def reference(tokens, cotangent, order, lengths, vectors, vector_moment, in_master, in_moment, in_error, in_factor, out_master, out_moment, out_error, out_factor):
    positions = jnp.arange(TOK_GRP, dtype=jnp.int32)

    def replica_step(totals, inputs):
        tok_rows, cot_rows, perm_row, length_row = inputs
        seq_ends = jnp.cumsum(length_row).astype(jnp.int32)
        segment = lax.optimization_barrier(jnp.sum((seq_ends[None, :] <= positions[:, None]).astype(jnp.int32), axis=1)).astype(jnp.int32)
        segment_pad = jnp.concatenate([jnp.full((CONV - 1,), -1, jnp.int32), segment]).astype(jnp.int32)
        stream = jnp.take(tok_rows, perm_row, axis=0).astype(jnp.float32)
        cot_packed = jnp.take(cot_rows, perm_row, axis=0).astype(jnp.float32)

        def replica_forward(vector_in, weight_in, weight_out, stream_in):
            return forward(vector_in, weight_in, weight_out, stream_in, segment_pad)
        result, pullback = jax.vjp(replica_forward, vectors, in_master, out_master, stream)
        grad_vec, grad_in, grad_out, grad_stream = pullback(cot_packed)
        inverse = jnp.zeros((TOK_GRP,), jnp.int32).at[perm_row].set(positions)
        mixed_rows = jnp.take(result, inverse, axis=0).astype(jnp.bfloat16)
        input_rows = jnp.take(grad_stream, inverse, axis=0).astype(jnp.bfloat16)
        return (totals + grad_vec, (mixed_rows, input_rows, grad_in, grad_out))
    vec_total, outs_all = lax.scan(replica_step, jnp.zeros_like(vectors), (tokens, cotangent, order, lengths))
    mixed, input_grad, in_grad, out_grad = outs_all
    replicas = tokens.shape[0]
    vector_grad = vec_total / replicas
    in_new, in_moment_new, in_error_new, in_factor_new = compress_update(in_grad, in_error, in_factor, in_moment, in_master, replicas)
    out_new, out_moment_new, out_error_new, out_factor_new = compress_update(out_grad, out_error, out_factor, out_moment, out_master, replicas)
    vector_moment_new = momentum_decay * vector_moment + vector_grad
    vector_new = vectors - vector_rate * vector_moment_new
    return (mixed, input_grad, in_grad, out_grad, vector_grad, in_new, in_moment_new, in_error_new, in_factor_new, out_new, out_moment_new, out_error_new, out_factor_new, vector_new, vector_moment_new)
```

```python
from functools import partial

import jax
import jax.numpy as jnp
import numpy as np
from jax import lax
from jax.experimental import pallas as pl
from jax.experimental.pallas import tpu as pltpu
from jax.sharding import PartitionSpec as P

D = 1024
HEADS = 32
HEADDIM = 64
STATE = 128
CONV = 4
BLOCK = 256
INNER = 2048
XBC = 2304
LANES = 128
REACH = CONV - 1

epsilon = 1e-05
momentum_decay = 0.9
weight_rate = 0.001
vector_rate = 0.02
highest = lax.Precision.HIGHEST
f32 = jnp.float32
bf16 = jnp.bfloat16
LOG2E = float(np.log2(np.e))


def nn(a, b):
    return lax.dot_general(a, b, (((1,), (0,)), ((), ())), preferred_element_type=f32)


def nt(a, b):
    return lax.dot_general(a, b, (((1,), (1,)), ((), ())), preferred_element_type=f32)


def tn(a, b):
    return lax.dot_general(a, b, (((0,), (0,)), ((), ())), preferred_element_type=f32)


def sigmoid(x):
    return 0.5 * jnp.tanh(0.5 * x) + 0.5


def pack3(x, width):
    hi = x.astype(bf16).astype(f32)
    rest = x - hi
    mid = rest.astype(bf16).astype(f32)
    low = rest - mid
    return (hi + pltpu.roll(mid, width, 1) + pltpu.roll(low, 2 * width, 1)).astype(bf16)


def unpack3(x, width):
    return x + pltpu.roll(x, LANES - width, 1) + pltpu.roll(x, LANES - 2 * width, 1)


def block_parts(heads, place, ends, x_ext, dt_raw, convw, small, wide, spread, tri):
    inner = heads * HEADDIM
    first = place * BLOCK
    column = first + lax.broadcasted_iota(jnp.int32, (BLOCK, 1), 0)
    row = first + lax.broadcasted_iota(jnp.int32, (1, BLOCK), 1)

    def segment(pos):
        total = jnp.zeros_like(pos)
        for k in range(ends.shape[0]):
            total = total + (ends[k] <= pos).astype(jnp.int32)
        return jnp.where(pos >= 0, total, -1)

    seg = segment(column)
    reach = [None] + [(segment(column - d) == seg).astype(f32) for d in range(1, CONV)]
    acc = convw[CONV : CONV + 1] + convw[REACH : REACH + 1] * x_ext[8:]
    for d in range(1, CONV):
        acc = acc + convw[REACH - d : CONV - d] * (x_ext[8 - d : 8 - d + BLOCK] * reach[d])
    sig = sigmoid(acc)
    mixed = (acc * sig).astype(bf16)
    values = mixed[:, :inner].astype(f32)
    write_keys = mixed[:, inner : inner + STATE]
    read_keys = mixed[:, inner + STATE :]

    lane = lax.broadcasted_iota(jnp.int32, (BLOCK, LANES), 1)
    live = lane < heads
    shifted = dt_raw + small[0:1]
    step = jnp.where(live, jnp.maximum(shifted, 0.0) + jnp.log1p(jnp.exp(-jnp.abs(shifted))), 0.0)
    log_decay = -small[1:2] * step
    cum = jnp.where(live, unpack3(nn(tri, pack3(log_decay, heads)), heads), 0.0) * LOG2E
    cum_rows = jnp.transpose(cum)
    enters = (seg == segment(column * 0 + (first - 1))).astype(f32)
    leaves = (seg == segment(column * 0 + (first + BLOCK - 1))).astype(f32)
    carry = jnp.where(live, jnp.exp2(cum) * enters, 0.0)
    tail = jnp.where(live, jnp.exp2(cum[BLOCK - 1 :] - cum) * leaves, 0.0)

    def expand(x):
        return nn(pack3(x, heads), spread)

    step_wide, carry_wide, tail_wide = expand(step), expand(carry), expand(tail)
    scaled = values * step_wide
    same = (seg == segment(row)) & (column >= row)
    hidden = jnp.where(same, 0.0, -1e30)
    read_write = nt(read_keys, write_keys)
    return dict(
        acc=acc, sig=sig, values=values, write_keys=write_keys, read_keys=read_keys, live=live,
        shifted=shifted, step=step, log_decay=log_decay, cum=cum, cum_rows=cum_rows,
        carry_wide=carry_wide, tail_wide=tail_wide, step_wide=step_wide, scaled=scaled,
        hidden=hidden, read_write=read_write, reach=reach, segment=segment, column=column, seg=seg,
    )


def decay_of(part, h):
    return jnp.exp2(part["cum"][:, h : h + 1] - part["cum_rows"][h : h + 1, :] + part["hidden"])


def forward_kernel(heads, ends, proj, convw, small, wide, spread, tri, y, states, squares, halo, state):
    inner = heads * HEADDIM
    place = pl.program_id(0)

    @pl.when(place == 0)
    def _():
        halo[...] = jnp.zeros_like(halo)
        state[...] = jnp.zeros_like(state)

    x = proj[:, inner : 2 * inner + 2 * STATE].astype(f32)
    x_ext = jnp.concatenate([halo[...], x], axis=0)
    halo[...] = x[BLOCK - 8 :]
    dt_raw = proj[:, 2 * inner + 2 * STATE :].astype(f32)
    part = block_parts(
        heads, place, ends, x_ext, dt_raw, convw[...], small[...], wide[...], spread[...], tri[...]
    )
    states[0] = state[...]
    scaled = part["scaled"].astype(bf16)
    lane = lax.broadcasted_iota(jnp.int32, (BLOCK, LANES), 1)
    carried = part["carry_wide"] * nn(part["read_keys"], state[...].astype(bf16))
    total = None
    for pair in range(heads // 2):
        cols = slice(pair * LANES, (pair + 1) * LANES)
        halves = []
        for h in (2 * pair, 2 * pair + 1):
            tile = (decay_of(part, h) * part["read_write"]).astype(bf16)
            halves.append(nn(tile, scaled[:, cols]))
        local = jnp.where(lane < HEADDIM, halves[0], halves[1])
        out = local + carried[:, cols] + wide[0:1, cols] * part["values"][:, cols]
        y[:, cols] = out
        gate = proj[:, cols].astype(f32)
        gated = out * (gate * sigmoid(gate))
        total = gated * gated if total is None else total + gated * gated
    hi = total.astype(bf16)
    low = (total - hi.astype(f32)).astype(bf16)
    ones = jnp.ones((8, LANES), bf16)
    squares[...] = nt(ones, hi) + nt(ones, low)
    leaving = (part["tail_wide"] * part["scaled"]).astype(bf16)
    state[...] = part["carry_wide"][BLOCK - 1 :] * state[...] + tn(part["write_keys"], leaving)


def forward_call(heads, ends, proj, convw, small, wide, spread, tri):
    inner = heads * HEADDIM
    rows, width = proj.shape
    blocks = rows // BLOCK
    channels = inner + 2 * STATE

    def whole(a):
        return pl.BlockSpec(a.shape, lambda i: (0,) * a.ndim)

    return pl.pallas_call(
        partial(forward_kernel, heads),
        grid=(blocks,),
        out_shape=[
            jax.ShapeDtypeStruct((rows, inner), f32),
            jax.ShapeDtypeStruct((blocks, STATE, inner), f32),
            jax.ShapeDtypeStruct((8, rows), f32),
        ],
        in_specs=[
            pl.BlockSpec(memory_space=pltpu.SMEM),
            pl.BlockSpec((BLOCK, width), lambda i: (i, 0)),
            whole(convw), whole(small), whole(wide), whole(spread), whole(tri),
        ],
        out_specs=[
            pl.BlockSpec((BLOCK, inner), lambda i: (i, 0)),
            pl.BlockSpec((1, STATE, inner), lambda i: (i, 0, 0)),
            pl.BlockSpec((8, BLOCK), lambda i: (0, i)),
        ],
        scratch_shapes=[pltpu.VMEM((8, channels), f32), pltpu.VMEM((STATE, inner), f32)],
        compiler_params=pltpu.CompilerParams(vmem_limit_bytes=48 * 1024 * 1024),
        name="mixer_forward",
    )(ends, proj, convw, small, wide, spread, tri)


def backward_kernel(
    heads, blocks, ends, proj, before, dn, y, states, sums, convw, small, wide, spread, collapse, tri,
    d_proj, d_conv, d_small, d_wide, after, d_state,
):
    inner = heads * HEADDIM
    turn = pl.program_id(0)
    place = blocks - 1 - turn

    @pl.when(turn == 0)
    def _():
        after[...] = jnp.zeros_like(after)
        d_state[...] = jnp.zeros_like(d_state)
        d_conv[...] = jnp.zeros_like(d_conv)
        d_small[...] = jnp.zeros_like(d_small)
        d_wide[...] = jnp.zeros_like(d_wide)

    x = proj[:, inner : 2 * inner + 2 * STATE].astype(f32)
    prior = before[8:, inner : 2 * inner + 2 * STATE].astype(f32)
    prior = jnp.where(place > 0, prior, 0.0)
    x_ext = jnp.concatenate([prior, x], axis=0)
    dt_raw = proj[:, 2 * inner + 2 * STATE :].astype(f32)
    part = block_parts(
        heads, place, ends, x_ext, dt_raw, convw[...], small[...], wide[...], spread[...], tri[...]
    )
    values, scaled32 = part["values"], part["scaled"]
    read_keys, write_keys = part["read_keys"], part["write_keys"]
    carry_wide, tail_wide, step_wide = part["carry_wide"], part["tail_wide"], part["step_wide"]
    skip, gain = wide[0:1], wide[1:2]

    columns = jnp.transpose(sums[...])
    scale = lax.rsqrt(columns[:, 0:1] * (1.0 / INNER) + epsilon)
    pull = scale * scale * scale * columns[:, 1:2] * (1.0 / INNER)
    gate = proj[:, :inner].astype(f32)
    gate_sig = sigmoid(gate)
    silu = gate * gate_sig
    out = y[...]
    gated = out * silu
    grad = dn[...].astype(f32)
    d_gated = scale * (grad * gain) - gated * pull
    d_gain = jnp.sum(grad * gated * scale, axis=0, keepdims=True)
    d_out = d_gated * silu
    d_gate = d_gated * out * (gate_sig * (1.0 + gate * (1.0 - gate_sig)))
    d_proj[:, :inner] = d_gate.astype(bf16)

    state = states[0]
    d_leaving = d_state[...]
    d_leaving16 = d_leaving.astype(bf16)
    d_out16 = d_out.astype(bf16)
    scaled = scaled32.astype(bf16)
    d_carried = (carry_wide * d_out).astype(bf16)
    d_tail = tail_wide * nn(write_keys, d_leaving16)
    leaving = (tail_wide * scaled32).astype(bf16)
    d_write = nt(leaving, d_leaving16)
    d_read = nt(d_carried, state.astype(bf16))
    carry_last = carry_wide[BLOCK - 1 :]
    d_state[...] = carry_last * d_leaving + tn(read_keys, d_carried)

    lane = lax.broadcasted_iota(jnp.int32, (BLOCK, LANES), 1)
    d_rw = None
    pieces = []
    for pair in range(heads // 2):
        cols = slice(pair * LANES, (pair + 1) * LANES)
        halves = []
        for k, h in enumerate((2 * pair, 2 * pair + 1)):
            own = (lane < HEADDIM) if k == 0 else (lane >= HEADDIM)
            decay = decay_of(part, h)
            tile = (decay * part["read_write"]).astype(bf16)
            mine = jnp.where(own, d_out16[:, cols], jnp.zeros((), bf16))
            d_tile = nt(mine, scaled[:, cols]) * decay
            d_rw = d_tile if d_rw is None else d_rw + d_tile
            halves.append(tn(tile, d_out16[:, cols]))
        pieces.append(jnp.where(lane < HEADDIM, halves[0], halves[1]))
    d_scaled = jnp.concatenate(pieces, axis=1) + d_tail
    d_rw16 = d_rw.astype(bf16)
    d_read = d_read + nn(d_rw16, write_keys)
    d_write = d_write + tn(d_rw16, read_keys)

    def gather_heads(v):
        hi = v.astype(bf16)
        low = (v - hi.astype(f32)).astype(bf16)
        return nn(hi, collapse[...]) + nn(low, collapse[...])

    flow = d_out * (out - skip * values) - scaled32 * d_scaled
    last_flow = jnp.sum(scaled32 * d_tail, axis=0, keepdims=True) + carry_last * jnp.sum(
        d_leaving * state, axis=0, keepdims=True
    )
    rows = lax.broadcasted_iota(jnp.int32, (BLOCK, 1), 0)
    flow = flow + jnp.where(rows == BLOCK - 1, last_flow, 0.0)
    d_cum = gather_heads(flow)
    d_log = unpack3(tn(tri[...], pack3(d_cum, heads)), heads)
    d_log = jnp.where(part["live"], d_log, 0.0)
    d_step = gather_heads(d_scaled * values) - small[1:2] * d_log
    d_dt = jnp.where(part["live"], d_step * sigmoid(part["shifted"]), 0.0)
    d_proj[:, 2 * inner + 2 * STATE :] = d_dt.astype(bf16)
    d_small[0:1, :] += jnp.sum(d_dt, axis=0, keepdims=True)
    d_small[1:2, :] += jnp.sum(d_log * part["log_decay"], axis=0, keepdims=True)
    d_wide[0:1, :] += jnp.sum(d_out * values, axis=0, keepdims=True)
    d_wide[1:2, :] += d_gain

    d_values = d_scaled * step_wide + skip * d_out
    acc, sig = part["acc"], part["sig"]
    d_acc = jnp.concatenate([d_values, d_write, d_read], axis=1) * (
        sig * (1.0 + acc * (1.0 - sig))
    )
    d_ext = jnp.concatenate([d_acc, after[...]], axis=0)
    after[...] = d_acc[:8]
    d_x = convw[REACH : REACH + 1] * d_acc
    d_conv[REACH : REACH + 1, :] += jnp.sum(d_acc * x, axis=0, keepdims=True)
    d_conv[CONV : CONV + 1, :] += jnp.sum(d_acc, axis=0, keepdims=True)
    for d in range(1, CONV):
        ahead = (part["segment"](part["column"] + d) == part["seg"]).astype(f32)
        d_x = d_x + convw[REACH - d : CONV - d] * (d_ext[d : d + BLOCK] * ahead)
        d_conv[REACH - d : CONV - d, :] += jnp.sum(
            d_acc * (x_ext[8 - d : 8 - d + BLOCK] * part["reach"][d]), axis=0, keepdims=True
        )
    d_proj[:, inner : 2 * inner + 2 * STATE] = d_x.astype(bf16)


def backward_call(heads, ends, proj, dn, y, states, sums, convw, small, wide, spread, collapse, tri):
    inner = heads * HEADDIM
    rows, width = proj.shape
    blocks = rows // BLOCK
    channels = inner + 2 * STATE
    last = blocks - 1

    def whole(a):
        return pl.BlockSpec(a.shape, lambda i: (0,) * a.ndim)

    return pl.pallas_call(
        partial(backward_kernel, heads, blocks),
        grid=(blocks,),
        out_shape=[
            jax.ShapeDtypeStruct((rows, width), bf16),
            jax.ShapeDtypeStruct((8, channels), f32),
            jax.ShapeDtypeStruct((8, LANES), f32),
            jax.ShapeDtypeStruct((8, inner), f32),
        ],
        in_specs=[
            pl.BlockSpec(memory_space=pltpu.SMEM),
            pl.BlockSpec((BLOCK, width), lambda i: (last - i, 0)),
            pl.BlockSpec((16, width), lambda i: (jnp.maximum((last - i) * (BLOCK // 16) - 1, 0), 0)),
            pl.BlockSpec((BLOCK, inner), lambda i: (last - i, 0)),
            pl.BlockSpec((BLOCK, inner), lambda i: (last - i, 0)),
            pl.BlockSpec((1, STATE, inner), lambda i: (last - i, 0, 0)),
            pl.BlockSpec((8, BLOCK), lambda i: (0, last - i)),
            whole(convw), whole(small), whole(wide), whole(spread), whole(collapse), whole(tri),
        ],
        out_specs=[
            pl.BlockSpec((BLOCK, width), lambda i: (last - i, 0)),
            pl.BlockSpec((8, channels), lambda i: (0, 0)),
            pl.BlockSpec((8, LANES), lambda i: (0, 0)),
            pl.BlockSpec((8, inner), lambda i: (0, 0)),
        ],
        scratch_shapes=[pltpu.VMEM((8, channels), f32), pltpu.VMEM((STATE, inner), f32)],
        compiler_params=pltpu.CompilerParams(vmem_limit_bytes=48 * 1024 * 1024),
        name="mixer_backward",
    )(ends, proj, proj, dn, y, states, sums, convw, small, wide, spread, collapse, tri)


def greet(axes, sizes, place):
    total = int(np.prod(sizes))
    barrier = pltpu.get_barrier_semaphore()

    def hail(d, carry):
        pl.semaphore_signal(
            barrier, inc=1, device_id=coordinates(axes, sizes, lax.rem(place + d, total)),
            device_id_type=pl.DeviceIdType.MESH,
        )
        return carry

    lax.fori_loop(1, total, hail, 0)
    pl.semaphore_wait(barrier, total - 1)


def coordinates(axes, sizes, place):
    where = {}
    for axis, size in reversed(list(zip(axes, sizes))):
        where[axis] = lax.rem(place, size)
        place = place // size
    return where


def my_place(axes, sizes):
    place = 0
    for axis, size in zip(axes, sizes):
        place = place * size + lax.axis_index(axis)
    return place


def share_kernel(axes, sizes, x, total, slots, send_sem, recv_sem):
    count = int(np.prod(sizes))
    me = my_place(axes, sizes)
    greet(axes, sizes, me)
    slots[me] = x[...]

    def copy_to(other, slot):
        return pltpu.make_async_remote_copy(
            src_ref=x, dst_ref=slots.at[slot], send_sem=send_sem.at[other], recv_sem=recv_sem.at[slot],
            device_id=coordinates(axes, sizes, other), device_id_type=pl.DeviceIdType.MESH,
        )

    def send(d, carry):
        copy_to(lax.rem(me + d, count), me).start()
        return carry

    def receive(d, carry):
        other = lax.rem(me + d, count)
        copy_to(other, other).wait_recv()
        return carry

    def sent(d, carry):
        copy_to(lax.rem(me + d, count), me).wait_send()
        return carry

    lax.fori_loop(1, count, send, 0)
    lax.fori_loop(1, count, receive, 0)
    lax.fori_loop(1, count, sent, 0)
    total[...] = lax.fori_loop(1, count, lambda i, acc: acc + slots[i], slots[0])


def share_sum(x, axes, sizes, collective_id):
    count = int(np.prod(sizes))
    return pl.pallas_call(
        partial(share_kernel, axes, sizes),
        out_shape=jax.ShapeDtypeStruct(x.shape, f32),
        in_specs=[pl.BlockSpec(memory_space=pltpu.VMEM)],
        out_specs=pl.BlockSpec(memory_space=pltpu.VMEM),
        scratch_shapes=[
            pltpu.VMEM((count,) + x.shape, f32),
            pltpu.SemaphoreType.DMA((count,)),
            pltpu.SemaphoreType.DMA((count,)),
        ],
        compiler_params=pltpu.CompilerParams(collective_id=collective_id, has_side_effects=True),
        name="share_sum",
    )(x)


def reduce_kernel(axes, sizes, x, total, slots, mine, send_sem, recv_sem, send_back, recv_back):
    count = int(np.prod(sizes))
    me = my_place(axes, sizes)
    greet(axes, sizes, me)
    slots[me] = x[me]

    def copy_to(other, slot):
        return pltpu.make_async_remote_copy(
            src_ref=x.at[other], dst_ref=slots.at[slot],
            send_sem=send_sem.at[other], recv_sem=recv_sem.at[slot],
            device_id=coordinates(axes, sizes, other), device_id_type=pl.DeviceIdType.MESH,
        )

    def copy_back(other, slot):
        return pltpu.make_async_remote_copy(
            src_ref=mine, dst_ref=total.at[slot],
            send_sem=send_back.at[other], recv_sem=recv_back.at[slot],
            device_id=coordinates(axes, sizes, other), device_id_type=pl.DeviceIdType.MESH,
        )

    def each(action):
        def one(d, carry):
            action(lax.rem(me + d, count))
            return carry

        lax.fori_loop(1, count, one, 0)

    each(lambda other: copy_to(other, me).start())
    each(lambda other: copy_to(other, other).wait_recv())
    mine[...] = lax.fori_loop(1, count, lambda i, acc: acc + slots[i], slots[0])
    total[me] = mine[...]
    each(lambda other: copy_back(other, me).start())
    each(lambda other: copy_to(other, me).wait_send())
    each(lambda other: copy_back(other, other).wait_recv())
    each(lambda other: copy_back(other, me).wait_send())


def reduce_sum(x, axes, sizes, collective_id):
    count = int(np.prod(sizes))
    return pl.pallas_call(
        partial(reduce_kernel, axes, sizes),
        out_shape=jax.ShapeDtypeStruct(x.shape, f32),
        in_specs=[pl.BlockSpec(memory_space=pltpu.VMEM)],
        out_specs=pl.BlockSpec(memory_space=pltpu.VMEM),
        scratch_shapes=[
            pltpu.VMEM(x.shape, f32),
            pltpu.VMEM(x.shape[1:], f32),
            pltpu.SemaphoreType.DMA((count,)),
            pltpu.SemaphoreType.DMA((count,)),
            pltpu.SemaphoreType.DMA((count,)),
            pltpu.SemaphoreType.DMA((count,)),
        ],
        compiler_params=pltpu.CompilerParams(collective_id=collective_id, has_side_effects=True),
        name="reduce_sum",
    )(x)


def assemble_kernel(group, heads, me, error, *refs):
    parts, (grad, merged) = refs[:group], refs[group:]
    inner = heads * HEADDIM
    shared = 2 * inner
    steps = shared + 2 * STATE
    keys, rates = None, None
    for k in range(group):
        owner = me[0] ^ k
        for piece in range(2):
            start = pl.multiple_of(piece * INNER + owner * inner, inner)
            grad[:, pl.ds(start, inner)] = parts[k][:, piece * inner : (piece + 1) * inner].astype(f32)
        part = parts[k][:, shared:steps].astype(f32)
        keys = part if keys is None else keys + part
        part = pltpu.roll(parts[k][:, steps:].astype(f32), owner * heads, 1)
        rates = part if rates is None else rates + part
    grad[:, 2 * INNER : 2 * INNER + 2 * STATE] = keys
    grad[:, 2 * INNER + 2 * STATE :] = rates[:, :HEADS]
    total = grad[...] + error[...]
    merged[...] = total


def assemble(heads, me, error, parts):
    group = len(parts)
    rows, columns = error.shape
    step = 64
    width = parts[0].shape[1]
    wide = pl.BlockSpec((step, columns), lambda i: (i, 0))
    return pl.pallas_call(
        partial(assemble_kernel, group, heads),
        grid=(rows // step,),
        out_shape=[jax.ShapeDtypeStruct((rows, columns), f32)] * 2,
        in_specs=[pl.BlockSpec(memory_space=pltpu.SMEM), wide]
        + [pl.BlockSpec((step, width), lambda i: (i, 0))] * group,
        out_specs=[wide] * 2,
        compiler_params=pltpu.CompilerParams(vmem_limit_bytes=48 * 1024 * 1024),
        name="assemble",
    )(me, error, *parts)


def split_vectors(vectors):
    widths = [D, CONV * XBC, XBC, HEADS, HEADS, HEADS, INNER]
    pieces = []
    offset = 0
    for span_size in widths:
        pieces.append(vectors[offset : offset + span_size])
        offset = offset + span_size
    norm_gain, conv_flat, conv_bias, dt_bias, decay_log, skip_gain, gate_gain = pieces
    return (
        norm_gain,
        conv_flat.reshape(CONV, XBC),
        conv_bias,
        dt_bias,
        decay_log,
        skip_gain,
        gate_gain,
    )


def spread_of(heads):
    lanes = np.arange(LANES)[:, None]
    return np.where(
        (lanes < 3 * heads) & (lanes % heads == np.arange(heads * HEADDIM)[None] // HEADDIM), 1.0, 0.0
    )


def collapse_of(heads):
    return np.where(np.arange(heads * HEADDIM)[:, None] // HEADDIM == np.arange(LANES)[None], 1.0, 0.0)


def local(
    tokens,
    cotangent,
    order,
    lengths,
    vectors,
    vector_moment,
    in_master,
    in_moment,
    in_error,
    in_factor,
    out_master,
    out_moment,
    out_error,
    out_factor,
):
    replicas = lax.axis_size("rep")
    group = lax.axis_size("grp")
    me = lax.axis_index("grp")
    heads = HEADS // group
    inner = INNER // group
    keys = 2 * STATE
    in_rows = in_master.shape[0]

    norm_gain, conv_weight, conv_bias, dt_bias, decay_log, skip_gain, gate_gain = split_vectors(vectors)

    def swap(x, k):
        return lax.ppermute(x, "grp", [(i, i ^ k) for i in range(group)])

    in16 = in_master.astype(bf16)

    def parcel(owner):
        return jnp.concatenate(
            [
                lax.dynamic_slice_in_dim(in16, owner * inner, inner, axis=1),
                lax.dynamic_slice_in_dim(in16, INNER + owner * inner, inner, axis=1),
                in16[:, 2 * INNER : 2 * INNER + keys],
                jnp.pad(
                    lax.dynamic_slice_in_dim(
                        in16, 2 * INNER + keys + owner * heads, heads, axis=1
                    ),
                    ((0, 0), (0, LANES - heads)),
                ),
            ],
            axis=1,
        )

    weight = jnp.zeros((group, in_rows, 2 * inner + keys + LANES), bf16)
    for k in range(group):
        piece = parcel(me ^ k)
        piece = swap(piece, k) if k else piece
        weight = lax.dynamic_update_index_in_dim(weight, piece, me ^ k, 0)
    width = weight.shape[2]
    weight = weight.reshape(group * in_rows, width)

    stream = tokens[0].astype(f32)
    inv_rms = lax.rsqrt(jnp.mean(stream * stream, axis=-1, keepdims=True) + epsilon)
    normed_own = (stream * inv_rms * norm_gain).astype(bf16)
    normed_parts = [normed_own] + [swap(normed_own, k) for k in range(1, group)]
    normed = jnp.concatenate(normed_parts, axis=0)
    cot_own, normed = lax.optimization_barrier((cotangent[0], normed))
    cot_all = jnp.concatenate([cot_own] + [swap(cot_own, k) for k in range(1, group)], axis=0)
    positions = order.shape[1]
    rows = positions // group
    slots = ((order[0] // rows) ^ me) * rows + order[0] % rows
    onehot = (slots[:, None] == lax.broadcasted_iota(jnp.int32, (1, positions), 1)).astype(bf16)

    ends = jnp.cumsum(lengths[0]).astype(jnp.int32)

    def own(a, size):
        return lax.dynamic_slice_in_dim(a, me * size, size, axis=a.ndim - 1)

    conv_all = jnp.concatenate([conv_weight, conv_bias[None]], axis=0)
    convw = jnp.concatenate([own(conv_all[:, :INNER], inner), conv_all[:, INNER:]], axis=1)
    convw = jnp.pad(convw, ((0, 8 - CONV - 1), (0, 0)))
    small = jnp.stack([own(dt_bias, heads), own(jnp.exp(decay_log), heads)])
    small = jnp.pad(small, ((0, 6), (0, LANES - heads)))
    own_gain = own(gate_gain, inner)
    wide = jnp.stack([jnp.repeat(own(skip_gain, heads), HEADDIM), own_gain])
    wide = jnp.pad(wide, ((0, 6), (0, 0)))
    spread = jnp.asarray(spread_of(heads), bf16)
    collapse = jnp.asarray(collapse_of(heads), bf16)
    tri = jnp.asarray(np.tril(np.ones((BLOCK, BLOCK))), bf16)

    proj_given = nn(normed, weight).astype(bf16)
    proj = nn(onehot, proj_given).astype(bf16)
    y, states, squares = forward_call(heads, ends, proj, convw, small, wide, spread, tri)

    out16 = out_master.astype(bf16)
    dn_given = nt(cot_all, out16).astype(bf16)
    dn = nn(onehot, dn_given).astype(bf16)
    gate = proj[:, :inner].astype(f32)
    gated = y * (gate * jax.nn.sigmoid(gate))
    leans = jnp.sum(dn.astype(f32) * own_gain * gated, axis=1)
    sums = jnp.stack([squares[0], leans])
    sums = sums + sum(swap(sums, k) for k in range(1, group))
    scale = lax.rsqrt(sums[0] / INNER + epsilon)
    normed_out = (gated * scale[:, None] * own_gain).astype(bf16)
    normed_given = tn(onehot, normed_out).astype(bf16)
    result_part = nn(normed_given, out16).reshape(group, rows, D)
    result = stream + result_part[0]
    for k in range(1, group):
        result = result + swap(result_part[k].astype(bf16), k).astype(f32)
    mixed_rows = result.astype(bf16)[None]
    out_owned = tn(normed_given, cot_all)

    sums8 = jnp.pad(sums, ((0, 6), (0, 0)))
    d_proj, d_conv, d_small, d_wide = backward_call(
        heads, ends, proj, dn, y, states, sums8, convw, small, wide, spread, collapse, tri
    )
    d_proj_given = tn(onehot, d_proj).astype(bf16)
    in_part16 = tn(normed, d_proj_given).astype(bf16).reshape(group, in_rows, width)
    sent = [lax.dynamic_index_in_dim(in_part16, me ^ k, 0, False) for k in range(group)]
    in_parts = sent[:1] + [swap(sent[k], k) for k in range(1, group)]
    in_owned, in_merged = assemble(heads, jnp.reshape(me, (1,)), in_error[0], in_parts)
    d_normed_part = nt(d_proj_given, weight)
    d_norm_gain = jnp.sum(d_normed_part * normed.astype(f32), axis=0) / norm_gain
    d_normed_part, in_owned = lax.optimization_barrier((d_normed_part, in_owned))
    d_normed_part = d_normed_part.reshape(group, rows, D)
    d_normed = d_normed_part[0]
    for k in range(1, group):
        d_normed = d_normed + swap(d_normed_part[k].astype(bf16), k).astype(f32)
    scaled = d_normed * norm_gain
    lean = jnp.mean(scaled * stream, axis=-1, keepdims=True)
    d_stream = inv_rms * scaled - stream * (inv_rms * inv_rms * inv_rms * lean)
    input_rows = (cotangent[0].astype(f32) + d_stream).astype(bf16)[None]

    def placed(a, total):
        size = a.shape[-1]
        zero = jnp.zeros(a.shape[:-1] + (total,), f32)
        return lax.dynamic_update_slice_in_dim(zero, a, me * size, axis=a.ndim - 1)

    d_conv_all = jnp.concatenate([placed(d_conv[:5, :inner], INNER), d_conv[:5, inner:]], axis=1)
    d_skip = jnp.sum(d_wide[0].reshape(heads, HEADDIM), axis=1)
    vector_local = jnp.concatenate(
        [
            d_norm_gain,
            d_conv_all[:CONV].reshape(-1),
            d_conv_all[CONV],
            placed(d_small[0, :heads], HEADS),
            placed(d_small[1, :heads], HEADS),
            placed(d_skip, HEADS),
            placed(d_wide[1], INNER),
        ]
    )

    out_merged = out_owned + out_error[0]

    def exact(a, b, dims):
        return lax.dot_general(a, b, (dims, ((), ())), precision=highest, preferred_element_type=f32)

    left = jnp.concatenate(
        [exact(in_factor, in_merged, ((0,), (1,))), exact(out_factor, out_merged, ((0,), (1,)))], axis=1
    )
    left = share_sum(left, ("rep",), (replicas,), 1)
    in_left, out_left = left[:, :in_rows], left[:, in_rows:]
    rank = left.shape[0]
    grams = jnp.concatenate([exact(in_left, in_left, ((1,), (1,))), exact(out_left, out_left, ((1,), (1,)))], axis=1)
    bundle = [
        exact(in_left, in_merged, ((1,), (0,))),
        exact(out_left, out_merged, ((1,), (0,))),
        grams,
        jnp.pad(vector_local, (0, -vector_local.size % rank)).reshape(rank, -1),
    ]
    bundle = [jnp.pad(b, ((0, 0), (0, -b.shape[1] % LANES))) for b in bundle]
    edges = np.cumsum([0] + [b.shape[1] for b in bundle])
    devices = group * replicas
    share = -(-int(edges[-1]) // (devices * LANES)) * LANES
    packed = jnp.pad(jnp.concatenate(bundle, axis=1), ((0, 0), (0, devices * share - int(edges[-1]))))
    packed = jnp.swapaxes(packed.reshape(rank, devices, share), 0, 1)
    packed = reduce_sum(packed, ("grp", "rep"), (group, replicas), 2)
    packed = jnp.swapaxes(packed, 0, 1).reshape(rank, devices * share)
    in_right, out_right, grams, vector_sum = [
        packed[:, edges[i] : edges[i + 1]] for i in range(4)
    ]
    columns = -(-vectors.shape[0] // rank)
    vector_grad = vector_sum[:, :columns].reshape(-1)[: vectors.shape[0]] / replicas

    def settle(gram, left_t, right_t, merged, moment, master):
        inverse = lax.linalg.triangular_solve(
            jnp.linalg.cholesky(gram / replicas), jnp.eye(rank, dtype=f32), left_side=True, lower=True
        )
        basis_t = exact(inverse, left_t, ((1,), (0,)))
        new_right = exact(inverse, right_t, ((1,), (0,))) / replicas
        approx = exact(basis_t, new_right, ((0,), (0,)))
        moment_new = momentum_decay * moment + approx
        return master - weight_rate * moment_new, moment_new, (merged - approx)[None], new_right.T

    in_new, in_moment_new, in_error_new, in_right = settle(
        grams[:, :rank], in_left, in_right[:, : in_master.shape[1]], in_merged, in_moment, in_master
    )
    out_new, out_moment_new, out_error_new, out_right = settle(
        grams[:, rank : 2 * rank], out_left, out_right[:, : out_master.shape[1]], out_merged, out_moment, out_master
    )
    vector_moment_new = momentum_decay * vector_moment + vector_grad
    vector_new = vectors - vector_rate * vector_moment_new
    return (
        mixed_rows,
        input_rows,
        in_owned[None],
        out_owned[None],
        vector_grad,
        in_new,
        in_moment_new,
        in_error_new,
        in_right,
        out_new,
        out_moment_new,
        out_error_new,
        out_right,
        vector_new,
        vector_moment_new,
    )


def solution(mesh):
    placed = (
        P("rep", "grp", None),
        P("rep", "grp", None),
        P("rep", None),
        P("rep", None),
        P(),
        P(),
        P("grp", None),
        P("grp", None),
        P("rep", "grp", None),
        P(),
        P("grp", None),
        P("grp", None),
        P("rep", "grp", None),
        P(),
    )
    return jax.shard_map(
        local,
        mesh=mesh,
        in_specs=placed,
        out_specs=(
            P("rep", "grp", None),
            P("rep", "grp", None),
            P("rep", "grp", None),
            P("rep", "grp", None),
            P(),
            P("grp", None),
            P("grp", None),
            P("rep", "grp", None),
            P(),
            P("grp", None),
            P("grp", None),
            P("rep", "grp", None),
            P(),
            P(),
            P(),
        ),
        check_vma=False,
    )
```

```python
from functools import partial
import jax
import jax.numpy as jnp
import numpy as np
from jax import lax
from jax.experimental import pallas as pl
from jax.experimental.pallas import tpu as pltpu
from jax.sharding import PartitionSpec as P
D = 1024
HEADS = 32
HEADDIM = 64
STATE = 128
CONV = 4
BLOCK = 256
INNER = 2048
XBC = 2304
LANES = 128
REACH = CONV - 1
epsilon = 1e-05
momentum_decay = 0.9
weight_rate = 0.001
vector_rate = 0.02
highest = lax.Precision.HIGHEST
f32 = jnp.float32
bf16 = jnp.bfloat16
LOG2E = float(np.log2(np.e))


def nn(a, b):
    return lax.dot_general(a, b, (((1,), (0,)), ((), ())), preferred_element_type=f32)


def nt(a, b):
    return lax.dot_general(a, b, (((1,), (1,)), ((), ())), preferred_element_type=f32)


def tn(a, b):
    return lax.dot_general(a, b, (((0,), (0,)), ((), ())), preferred_element_type=f32)


def sigmoid(x):
    return 0.5 * jnp.tanh(0.5 * x) + 0.5


def pack3(x, width):
    hi = x.astype(bf16).astype(f32)
    rest = x - hi
    mid = rest.astype(bf16).astype(f32)
    low = rest - mid
    return (hi + pltpu.roll(mid, width, 1) + pltpu.roll(low, 2 * width, 1)).astype(bf16)


def unpack3(x, width):
    return x + pltpu.roll(x, LANES - width, 1) + pltpu.roll(x, LANES - 2 * width, 1)


def block_parts(heads, place, ends, x_ext, dt_raw, convw, small, wide, spread, tri):
    inner = heads * HEADDIM
    first = place * BLOCK
    column = first + lax.broadcasted_iota(jnp.int32, (BLOCK, 1), 0)
    row = first + lax.broadcasted_iota(jnp.int32, (1, BLOCK), 1)

    def segment(pos):
        total = jnp.zeros_like(pos)
        for k in range(ends.shape[0]):
            total = total + (ends[k] <= pos).astype(jnp.int32)
        return jnp.where(pos >= 0, total, -1)

    seg = segment(column)
    reach = [None] + [(segment(column - d) == seg).astype(f32) for d in range(1, CONV)]
    acc = convw[CONV : CONV + 1] + convw[REACH : REACH + 1] * x_ext[8:]
    for d in range(1, CONV):
        acc = acc + convw[REACH - d : CONV - d] * (x_ext[8 - d : 8 - d + BLOCK] * reach[d])
    sig = sigmoid(acc)
    mixed = (acc * sig).astype(bf16)
    values = mixed[:, :inner].astype(f32)
    write_keys = mixed[:, inner : inner + STATE]
    read_keys = mixed[:, inner + STATE :]

    lane = lax.broadcasted_iota(jnp.int32, (BLOCK, LANES), 1)
    live = lane < heads
    shifted = dt_raw + small[0:1]
    step = jnp.where(live, jnp.maximum(shifted, 0.0) + jnp.log1p(jnp.exp(-jnp.abs(shifted))), 0.0)
    log_decay = -small[1:2] * step
    cum = jnp.where(live, unpack3(nn(tri, pack3(log_decay, heads)), heads), 0.0) * LOG2E
    cum_rows = jnp.transpose(cum)
    enters = (seg == segment(column * 0 + (first - 1))).astype(f32)
    leaves = (seg == segment(column * 0 + (first + BLOCK - 1))).astype(f32)
    carry = jnp.where(live, jnp.exp2(cum) * enters, 0.0)
    tail = jnp.where(live, jnp.exp2(cum[BLOCK - 1 :] - cum) * leaves, 0.0)

    def expand(x):
        return nn(pack3(x, heads), spread)

    step_wide, carry_wide, tail_wide = expand(step), expand(carry), expand(tail)
    scaled = values * step_wide
    same = (seg == segment(row)) & (column >= row)
    hidden = jnp.where(same, 0.0, -1e30)
    read_write = nt(read_keys, write_keys)
    return dict(
        acc=acc, sig=sig, values=values, write_keys=write_keys, read_keys=read_keys, live=live,
        shifted=shifted, step=step, log_decay=log_decay, cum=cum, cum_rows=cum_rows,
        carry_wide=carry_wide, tail_wide=tail_wide, step_wide=step_wide, scaled=scaled,
        hidden=hidden, read_write=read_write, reach=reach, segment=segment, column=column, seg=seg,
    )


def decay_of(part, h):
    return jnp.exp2(part["cum"][:, h : h + 1] - part["cum_rows"][h : h + 1, :] + part["hidden"])
PITCH = 16
HALF = 8
VMEM_LIMIT = 56 * 1024 * 1024


def store_rows(ref, base, value, pitch):
    count = value.shape[0]
    for c in range(value.shape[1] // LANES):
        ref[pl.ds(base * pitch + c, count, stride=pitch), :] = value[:, c * LANES : (c + 1) * LANES]


def load_rows(ref, base, count, chunks, pitch):
    return jnp.concatenate(
        [ref[pl.ds(base * pitch + c, count, stride=pitch), :] for c in range(chunks)], axis=1
    )


def gather_rows(order, first, source, target, pitch):
    def some(i, carry):
        for u in range(8):
            row = order[0, first + i * 8 + u] * pitch
            target[pl.ds(pl.multiple_of((i * 8 + u) * pitch, pitch), pitch), :] = source[pl.ds(row, pitch), :]
        return carry

    lax.fori_loop(0, BLOCK // 8, some, 0)


def scatter_rows(order, first, source, target, pitch):
    def some(i, carry):
        for u in range(8):
            row = pl.multiple_of(order[0, first + i * 8 + u] * pitch, pitch)
            target[pl.ds(row, pitch), :] = source[pl.ds(pl.multiple_of((i * 8 + u) * pitch, pitch), pitch), :]
        return carry

    lax.fori_loop(0, BLOCK // 8, some, 0)


def row_sums(total):
    hi = total.astype(bf16)
    low = (total - hi.astype(f32)).astype(bf16)
    ones = jnp.ones((8, LANES), bf16)
    return nt(ones, hi) + nt(ones, low)


def fold(value):
    total = value[:, :LANES]
    for c in range(1, value.shape[1] // LANES):
        total = total + value[:, c * LANES : (c + 1) * LANES]
    return total


def whole(a):
    return pl.BlockSpec(a.shape, lambda i: (0,) * a.ndim)
SMEM = pl.BlockSpec(memory_space=pltpu.SMEM)


def front_kernel(
    heads, rows, ends, order, tokens, cotangent, master, out16, convw, small, wide, spread, tri,
    weight_out, normed_out, cot_out, proj_out, y_out, states_out, dn_out, sums_out,
    weight, normed, cot, given, packed, proj, y, states, dn, halo, state, sums, arrived,
    send, recv, keep, save,
):
    group = order.shape[1] // rows
    inner = heads * HEADDIM
    shared = 2 * inner + 2 * STATE
    positions = order.shape[1]
    blocks = positions // BLOCK
    in_cols = master.shape[1]
    me = lax.axis_index("grp")
    rep = lax.axis_index("rep")
    core = lax.rem(rep, 2)
    sibling = {"rep": rep + 1 - 2 * core}
    mesh_id = pl.DeviceIdType.MESH
    lane = lax.broadcasted_iota(jnp.int32, (BLOCK, LANES), 1)
    half = rows // 2

    barrier = pltpu.get_barrier_semaphore()
    for k in range(1, group):
        pl.semaphore_signal(barrier, inc=1, device_id={"grp": me ^ k}, device_id_type=mesh_id)
    pl.semaphore_signal(barrier, inc=1, device_id=sibling, device_id_type=mesh_id)

    pieces = [(0, 0, inner), (INNER, inner, inner), (2 * INNER, 2 * inner, 2 * STATE), (2 * INNER + 2 * STATE, shared, HEADS)]

    def remote(src, dst, index, target):
        return pltpu.make_async_remote_copy(
            src_ref=src, dst_ref=dst, send_sem=send.at[index], recv_sem=recv.at[index],
            device_id=target, device_id_type=mesh_id,
        )

    def columns(owner):
        return pl.ds(pl.multiple_of(owner * in_cols, in_cols), in_cols)

    def weight_copy(k, p, owner, reader):
        source, target, count = pieces[p]
        part = count // 2
        start = source + core * part + (reader * count if p < 2 else 0)
        return remote(
            master.at[pl.ds(pl.multiple_of(start, 16), part), :],
            weight.at[pl.ds(pl.multiple_of(target + core * part, 16), part), columns(owner)],
            4 * (k - 1) + p, {"grp": me ^ k},
        )

    def twin_copy(k, p, side):
        target, part = pieces[p][1], pieces[p][2] // 2
        where = weight.at[pl.ds(pl.multiple_of(target + side * part, 16), part), columns(me ^ k)]
        return remote(where, where, 12 + 4 * (k - 1) + p, sibling)

    def slot(ref, k, part=None):
        if part is None:
            return ref.at[pl.ds(k * rows, rows), :]
        return ref.at[pl.ds(k * rows + part * half, half), :]

    def row_copy(own, ref, k, base):
        return remote(own, slot(ref, k), base + k - 1, {"grp": me ^ k})

    def pass_copy(ref, k, base):
        return remote(slot(ref, k, k - 1), slot(ref, 3, k - 1), base + 1 + k, {"grp": me ^ (3 - k)})

    own = []
    for p in range(4):
        source, target, count = pieces[p]
        start = source + (me * count if p < 2 else 0)
        own.append(
            pltpu.make_async_copy(
                master.at[pl.ds(pl.multiple_of(start, 16), count), :],
                weight.at[pl.ds(target, count), columns(me)], keep.at[p],
            )
        )
    own.append(pltpu.make_async_copy(tokens, slot(normed, 0), keep.at[4]))
    own.append(pltpu.make_async_copy(cotangent, slot(cot, 0), keep.at[5]))
    for c in own:
        c.start()

    pl.semaphore_wait(barrier, group)
    for k in (1, 2, 3):
        for p in range(4):
            weight_copy(k, p, me, me ^ k).start()
    for k in (1, 2):
        row_copy(tokens, normed, k, 24).start()
    for k in (1, 2, 3):
        for p in range(4):
            weight_copy(k, p, me ^ k, me).wait_recv()
            twin_copy(k, p, core).start()
    for c in own:
        c.wait()
    for k in (1, 2, 3):
        for p in range(4):
            twin_copy(k, p, 1 - core).wait_recv()

    def project(k):
        def one(i, carry):
            first = pl.multiple_of(k * rows + i * BLOCK, BLOCK)
            x = normed[pl.ds(first, BLOCK), :]
            main = nt(x, weight[:shared, :]).astype(bf16).astype(f32)
            rates = nt(x, weight[shared:, :]).astype(bf16).astype(f32)
            rates = jnp.concatenate([rates, jnp.zeros((BLOCK, LANES - HEADS), f32)], axis=1)
            rates = pltpu.roll(rates, lax.rem(LANES - me * heads, LANES), 1)
            rates = jnp.where(lane < heads, rates, 0.0)
            store_rows(given, first, jnp.concatenate([main, rates], axis=1), PITCH)
            return carry

        lax.fori_loop(0, rows // BLOCK, one, 0)

    project(0)
    for k in (1, 2):
        row_copy(tokens, normed, k, 24).wait_recv()
        pass_copy(normed, k, 24).start()
    for k in (1, 2):
        row_copy(cotangent, cot, k, 28).start()
    project(1)
    project(2)
    for k in (1, 2):
        pass_copy(normed, k, 24).wait_recv()
    project(3)

    weight_save = pltpu.make_async_copy(weight, weight_out, save.at[0])
    normed_save = pltpu.make_async_copy(normed, normed_out, save.at[1])
    weight_save.start()
    normed_save.start()
    halo[...] = jnp.zeros_like(halo)
    state[...] = jnp.zeros_like(state)

    def scan(place, carry):
        @pl.when(place == blocks - 2)
        def _():
            for k in (1, 2):
                row_copy(cotangent, cot, k, 28).wait_recv()
                pass_copy(cot, k, 28).start()

        base = pl.multiple_of(place * BLOCK, BLOCK)
        gather_rows(order, base, given, packed, PITCH)
        x_all = load_rows(packed, 0, BLOCK, shared // LANES + 1, PITCH)
        proj[pl.ds(base, BLOCK), :] = x_all.astype(bf16)
        gate_all = x_all[:, :inner]
        x = x_all[:, inner:shared]
        x_ext = jnp.concatenate([halo[...], x], axis=0)
        halo[...] = x[BLOCK - 8 :]
        part = block_parts(
            heads, place, ends, x_ext, x_all[:, shared:], convw[...], small[...], wide[...], spread[...], tri[...]
        )
        states[place] = state[...]
        scaled = part["scaled"].astype(bf16)
        carried = part["carry_wide"] * nn(part["read_keys"], state[...].astype(bf16))
        total = None
        for pair in range(heads // 2):
            cols = slice(pair * LANES, (pair + 1) * LANES)
            halves = []
            for h in (2 * pair, 2 * pair + 1):
                tile = (decay_of(part, h) * part["read_write"]).astype(bf16)
                halves.append(nn(tile, scaled[:, cols]))
            local = jnp.where(lane < HEADDIM, halves[0], halves[1])
            out = local + carried[:, cols] + wide[0:1, cols] * part["values"][:, cols]
            y[pl.ds(base, BLOCK), cols] = out
            gate = gate_all[:, cols]
            gated = out * (gate * sigmoid(gate))
            total = gated * gated if total is None else total + gated * gated
        sums[0:8, pl.ds(base, BLOCK)] = row_sums(total)
        leaving = (part["tail_wide"] * part["scaled"]).astype(bf16)
        state[...] = part["carry_wide"][BLOCK - 1 :] * state[...] + tn(part["write_keys"], leaving)
        return carry

    lax.fori_loop(0, blocks, scan, 0)
    saves = [
        pltpu.make_async_copy(proj, proj_out, save.at[2]),
        pltpu.make_async_copy(y, y_out, save.at[3]),
        pltpu.make_async_copy(states, states_out, save.at[4]),
    ]
    for c in saves:
        c.start()

    def pull(k):
        def one(i, carry):
            first = pl.multiple_of(k * rows + i * BLOCK, BLOCK)
            store_rows(given, first, nt(cot[pl.ds(first, BLOCK), :], out16[...]), HALF)
            return carry

        lax.fori_loop(0, rows // BLOCK, one, 0)

    for k in range(3):
        pull(k)
    for k in (1, 2):
        pass_copy(cot, k, 28).wait_recv()
    pull(3)
    cot_save = pltpu.make_async_copy(cot, cot_out, save.at[5])
    cot_save.start()

    def lean(place, carry):
        base = pl.multiple_of(place * BLOCK, BLOCK)
        gather_rows(order, base, given, packed, HALF)
        grad = load_rows(packed, 0, BLOCK, inner // LANES, HALF)
        dn[pl.ds(base, BLOCK), :] = grad.astype(bf16)
        x = proj[pl.ds(base, BLOCK), :inner].astype(f32)
        gated = y[pl.ds(base, BLOCK), :] * (x * sigmoid(x))
        sums[8:16, pl.ds(base, BLOCK)] = row_sums(fold(grad * wide[1:2] * gated))
        return carry

    lax.fori_loop(0, blocks, lean, 0)
    dn_save = pltpu.make_async_copy(dn, dn_out, save.at[6])
    dn_save.start()

    def sums_copy(k):
        return remote(sums, arrived.at[k - 1], 31 + k, {"grp": me ^ k})

    for k in (1, 2, 3):
        sums_copy(k).start()
    for k in (1, 2, 3):
        sums_copy(k).wait_recv()
    sums_out[0:8, :] = sums[0:8, :] + arrived[0, 0:8, :] + arrived[1, 0:8, :] + arrived[2, 0:8, :]
    sums_out[8:16, :] = sums[8:16, :] + arrived[0, 8:16, :] + arrived[1, 8:16, :] + arrived[2, 8:16, :]

    for k in (1, 2, 3):
        sums_copy(k).wait_send()
        for p in range(4):
            weight_copy(k, p, me, me ^ k).wait_send()
            twin_copy(k, p, core).wait_send()
    for k in (1, 2):
        row_copy(tokens, normed, k, 24).wait_send()
        pass_copy(normed, k, 24).wait_send()
        row_copy(cotangent, cot, k, 28).wait_send()
        pass_copy(cot, k, 28).wait_send()
    for c in [weight_save, normed_save, cot_save, dn_save] + saves:
        c.wait()
VM = pl.BlockSpec(memory_space=pltpu.VMEM)
ANY = pl.BlockSpec(memory_space=pl.ANY)


def front_call(heads, ends, order, tokens, cotangent, master, out16, convw, small, wide, spread, tri):
    inner = heads * HEADDIM
    rows = tokens.shape[0]
    positions = order.shape[1]
    width = 2 * inner + 2 * STATE + LANES
    blocks = positions // BLOCK
    channels = inner + 2 * STATE
    weight = (2 * inner + 2 * STATE + HEADS, D)
    return pl.pallas_call(
        partial(front_kernel, heads, rows),
        out_shape=[
            jax.ShapeDtypeStruct(weight, bf16),
            jax.ShapeDtypeStruct((positions, D), bf16),
            jax.ShapeDtypeStruct((positions, D), bf16),
            jax.ShapeDtypeStruct((positions, width), bf16),
            jax.ShapeDtypeStruct((positions, inner), f32),
            jax.ShapeDtypeStruct((blocks, STATE, inner), f32),
            jax.ShapeDtypeStruct((positions, inner), bf16),
            jax.ShapeDtypeStruct((16, positions), f32),
        ],
        in_specs=[SMEM, SMEM, ANY, ANY, ANY] + [VM] * 6,
        out_specs=[ANY] * 7 + [VM],
        scratch_shapes=[
            pltpu.VMEM(weight, bf16),
            pltpu.VMEM((positions, D), bf16),
            pltpu.VMEM((positions, D), bf16),
            pltpu.VMEM((positions * PITCH, LANES), f32),
            pltpu.VMEM((BLOCK * PITCH, LANES), f32),
            pltpu.VMEM((positions, width), bf16),
            pltpu.VMEM((positions, inner), f32),
            pltpu.VMEM((blocks, STATE, inner), f32),
            pltpu.VMEM((positions, inner), bf16),
            pltpu.VMEM((8, channels), f32),
            pltpu.VMEM((STATE, inner), f32),
            pltpu.VMEM((16, positions), f32),
            pltpu.VMEM((3, 16, positions), f32),
            pltpu.SemaphoreType.DMA((35,)),
            pltpu.SemaphoreType.DMA((35,)),
            pltpu.SemaphoreType.DMA((6,)),
            pltpu.SemaphoreType.DMA((7,)),
        ],
        compiler_params=pltpu.CompilerParams(
            vmem_limit_bytes=60 * 1024 * 1024, collective_id=3, has_side_effects=True
        ),
        name="front",
    )(ends, order, tokens, cotangent, master, out16, convw, small, wide, spread, tri)


def norm_parts(sums):
    columns = jnp.transpose(sums)
    scale = lax.rsqrt(columns[:, 0:1] * (1.0 / INNER) + epsilon)
    return scale, scale * scale * scale * columns[:, 1:2] * (1.0 / INNER)


def gate_kernel(
    heads, blocks, order, gate, y, dn, sums, wide, cot, normed, out16,
    result, d_gate, out_grad, in_grad, d_gain, given, packed,
):
    inner = heads * HEADDIM
    turn = pl.program_id(0)

    @pl.when(turn < blocks)
    def _():
        scale, pull = norm_parts(sums[...])
        x = gate[...].astype(f32)
        sig = sigmoid(x)
        out = y[...]
        gated = out * (x * sig)
        grad = dn[...].astype(f32)
        gain = wide[1:2]
        normed_out = (gated * scale * gain).astype(bf16).astype(f32)
        d_gated = scale * (grad * gain) - gated * pull
        d_x = (d_gated * out * (sig * (1.0 + x * (1.0 - sig)))).astype(bf16).astype(f32)
        total = jnp.sum(grad * gated * scale, axis=0, keepdims=True)
        total = jnp.broadcast_to(total, d_gain.shape)
        d_gain[...] = jnp.where(turn == 0, total, d_gain[...] + total)
        store_rows(packed, 0, jnp.concatenate([normed_out, d_x], axis=1), HALF)
        scatter_rows(order, turn * BLOCK, packed, given, HALF)

    @pl.when(turn == blocks)
    def _():
        out_grad[...] = jnp.zeros_like(out_grad)
        in_grad[...] = jnp.zeros_like(in_grad)

    @pl.when(turn >= blocks)
    def _():
        both = load_rows(given, (turn - blocks) * BLOCK, BLOCK, 2 * inner // LANES, HALF).astype(bf16)
        left, right = both[:, :inner], both[:, inner:]
        result[...] = nn(left, out16[...]).astype(bf16)
        d_gate[...] = right
        out_grad[...] += tn(left, cot[...])
        in_grad[...] += tn(right, normed[...])


def gate_call(heads, order, proj, y, dn, sums, wide, cot, normed, out16):
    inner = heads * HEADDIM
    rows = cot.shape[0]
    blocks = rows // BLOCK

    def early(i):
        return jnp.minimum(i, blocks - 1)

    def late(i):
        return jnp.maximum(i - blocks, 0)

    return pl.pallas_call(
        partial(gate_kernel, heads, blocks),
        grid=(2 * blocks,),
        out_shape=[
            jax.ShapeDtypeStruct((rows, D), bf16),
            jax.ShapeDtypeStruct((rows, inner), bf16),
            jax.ShapeDtypeStruct((inner, D), f32),
            jax.ShapeDtypeStruct((inner, D), f32),
            jax.ShapeDtypeStruct((8, inner), f32),
        ],
        in_specs=[
            SMEM,
            pl.BlockSpec((BLOCK, inner), lambda i: (early(i), 0)),
            pl.BlockSpec((BLOCK, inner), lambda i: (early(i), 0)),
            pl.BlockSpec((BLOCK, inner), lambda i: (early(i), 0)),
            pl.BlockSpec((8, BLOCK), lambda i: (0, early(i))),
            whole(wide),
            pl.BlockSpec((BLOCK, D), lambda i: (late(i), 0)),
            pl.BlockSpec((BLOCK, D), lambda i: (late(i), 0)),
            whole(out16),
        ],
        out_specs=[
            pl.BlockSpec((BLOCK, D), lambda i: (late(i), 0)),
            pl.BlockSpec((BLOCK, inner), lambda i: (late(i), 0)),
            pl.BlockSpec((inner, D), lambda i: (0, 0)),
            pl.BlockSpec((inner, D), lambda i: (0, 0)),
            pl.BlockSpec((8, inner), lambda i: (0, 0)),
        ],
        scratch_shapes=[
            pltpu.VMEM((rows * HALF, LANES), f32),
            pltpu.VMEM((BLOCK * HALF, LANES), f32),
        ],
        compiler_params=pltpu.CompilerParams(vmem_limit_bytes=VMEM_LIMIT),
        cost_estimate=pl.CostEstimate(flops=6 * rows * D * inner, bytes_accessed=24_000_000, transcendentals=0),
        name="gate_back",
    )(order, proj, y, dn, sums, wide, cot, normed, out16)


def backward_block(
    heads, me, order, place, ends, proj, before, dn, y, states, sums, convw, small, wide, spread, collapse, tri,
    d_conv, d_small, d_skip, given, packed, after, d_state,
):
    inner = heads * HEADDIM

    x = proj[:, inner : 2 * inner + 2 * STATE].astype(f32)
    prior = before[8:, inner : 2 * inner + 2 * STATE].astype(f32)
    prior = jnp.where(place > 0, prior, 0.0)
    x_ext = jnp.concatenate([prior, x], axis=0)
    dt_raw = proj[:, 2 * inner + 2 * STATE :].astype(f32)
    part = block_parts(
        heads, place, ends, x_ext, dt_raw, convw[...], small[...], wide[...], spread[...], tri[...]
    )
    values, scaled32 = part["values"], part["scaled"]
    read_keys, write_keys = part["read_keys"], part["write_keys"]
    carry_wide, tail_wide, step_wide = part["carry_wide"], part["tail_wide"], part["step_wide"]
    skip, gain = wide[0:1], wide[1:2]

    scale, pull = norm_parts(sums[...])
    gate = proj[:, :inner].astype(f32)
    gate_sig = sigmoid(gate)
    silu = gate * gate_sig
    out = y[...]
    gated = out * silu
    grad = dn[...].astype(f32)
    d_gated = scale * (grad * gain) - gated * pull
    d_out = d_gated * silu
    state = states[0]
    d_leaving = d_state[...]
    d_leaving16 = d_leaving.astype(bf16)
    d_out16 = d_out.astype(bf16)
    scaled = scaled32.astype(bf16)
    d_carried = (carry_wide * d_out).astype(bf16)
    d_tail = tail_wide * nn(write_keys, d_leaving16)
    leaving = (tail_wide * scaled32).astype(bf16)
    d_write = nt(leaving, d_leaving16)
    d_read = nt(d_carried, state.astype(bf16))
    carry_last = carry_wide[BLOCK - 1 :]
    d_state[...] = carry_last * d_leaving + tn(read_keys, d_carried)

    lane = lax.broadcasted_iota(jnp.int32, (BLOCK, LANES), 1)
    d_rw = None
    pieces = []
    for pair in range(heads // 2):
        cols = slice(pair * LANES, (pair + 1) * LANES)
        halves = []
        for k, h in enumerate((2 * pair, 2 * pair + 1)):
            own = (lane < HEADDIM) if k == 0 else (lane >= HEADDIM)
            decay = decay_of(part, h)
            tile = (decay * part["read_write"]).astype(bf16)
            mine = jnp.where(own, d_out16[:, cols], jnp.zeros((), bf16))
            d_tile = nt(mine, scaled[:, cols]) * decay
            d_rw = d_tile if d_rw is None else d_rw + d_tile
            halves.append(tn(tile, d_out16[:, cols]))
        pieces.append(jnp.where(lane < HEADDIM, halves[0], halves[1]))
    d_scaled = jnp.concatenate(pieces, axis=1) + d_tail
    d_rw16 = d_rw.astype(bf16)
    d_read = d_read + nn(d_rw16, write_keys)
    d_write = d_write + tn(d_rw16, read_keys)

    def gather_heads(v):
        hi = v.astype(bf16)
        low = (v - hi.astype(f32)).astype(bf16)
        return nn(hi, collapse[...]) + nn(low, collapse[...])

    flow = d_out * (out - skip * values) - scaled32 * d_scaled
    last_flow = jnp.sum(scaled32 * d_tail, axis=0, keepdims=True) + carry_last * jnp.sum(
        d_leaving * state, axis=0, keepdims=True
    )
    rows = lax.broadcasted_iota(jnp.int32, (BLOCK, 1), 0)
    flow = flow + jnp.where(rows == BLOCK - 1, last_flow, 0.0)
    d_cum = gather_heads(flow)
    d_log = unpack3(tn(tri[...], pack3(d_cum, heads)), heads)
    d_log = jnp.where(part["live"], d_log, 0.0)
    d_step = gather_heads(d_scaled * values) - small[1:2] * d_log
    d_dt = jnp.where(part["live"], d_step * sigmoid(part["shifted"]), 0.0)
    d_small[0:1, :] += jnp.sum(d_dt, axis=0, keepdims=True)
    d_small[1:2, :] += jnp.sum(d_log * part["log_decay"], axis=0, keepdims=True)
    d_skip[0:1, :] += jnp.sum(d_out * values, axis=0, keepdims=True)

    d_values = d_scaled * step_wide + skip * d_out
    acc, sig = part["acc"], part["sig"]
    d_acc = jnp.concatenate([d_values, d_write, d_read], axis=1) * (
        sig * (1.0 + acc * (1.0 - sig))
    )
    d_ext = jnp.concatenate([d_acc, after[...]], axis=0)
    after[...] = d_acc[:8]
    d_x = convw[REACH : REACH + 1] * d_acc
    d_conv[REACH : REACH + 1, :] += jnp.sum(d_acc * x, axis=0, keepdims=True)
    d_conv[CONV : CONV + 1, :] += jnp.sum(d_acc, axis=0, keepdims=True)
    for d in range(1, CONV):
        ahead = (part["segment"](part["column"] + d) == part["seg"]).astype(f32)
        d_x = d_x + convw[REACH - d : CONV - d] * (d_ext[d : d + BLOCK] * ahead)
        d_conv[REACH - d : CONV - d, :] += jnp.sum(
            d_acc * (x_ext[8 - d : 8 - d + BLOCK] * part["reach"][d]), axis=0, keepdims=True
        )
    d_rates = pltpu.roll(d_dt, me[0] * heads, 1)
    d_all = jnp.concatenate([d_x, d_rates], axis=1).astype(bf16).astype(f32)
    store_rows(packed, 0, d_all, HALF)
    scatter_rows(order, place * BLOCK, packed, given, HALF)


def backward_kernel(
    heads, blocks, me, ends, order, proj, before, dn, y, states, sums, convw, small, wide, spread, collapse,
    tri, d_gate, normed, weight,
    d_normed, in_grad, d_norm_gain, d_conv, d_small, d_skip, given, packed, after, d_state, total,
):
    inner = heads * HEADDIM
    shared = 2 * inner + 2 * STATE
    turn = pl.program_id(0)

    @pl.when(turn == 0)
    def _():
        after[...] = jnp.zeros_like(after)
        d_state[...] = jnp.zeros_like(d_state)
        d_conv[...] = jnp.zeros_like(d_conv)
        d_small[...] = jnp.zeros_like(d_small)
        d_skip[...] = jnp.zeros_like(d_skip)
        d_norm_gain[...] = jnp.zeros_like(d_norm_gain)
        total[...] = jnp.zeros_like(total)

    @pl.when(turn < blocks)
    def _():
        backward_block(
            heads, me, order, blocks - 1 - turn, ends, proj, before, dn, y, states, sums, convw, small, wide,
            spread, collapse, tri, d_conv, d_small, d_skip, given, packed, after, d_state,
        )

    @pl.when(turn >= blocks)
    def _():
        chunks = (shared - inner) // LANES + 1
        grad = load_rows(given, (turn - blocks) * BLOCK, BLOCK, chunks, HALF).astype(bf16)
        rates = grad[:, shared - inner : shared - inner + HEADS]
        rows = normed[...]
        total[...] += tn(grad, rows)
        back = nn(grad[:, : shared - inner], weight[inner:shared, :])
        back = back + nn(d_gate[...], weight[:inner, :]) + nn(rates, weight[shared:, :])
        d_normed[...] = back.astype(bf16)
        d_norm_gain[0:1, :] += jnp.sum(back * rows.astype(f32), axis=0, keepdims=True)

    @pl.when(turn == 2 * blocks - 1)
    def _():
        in_grad[...] = total[: shared - inner + HEADS, :].astype(bf16)


def backward_call(
    heads, me, ends, order, proj, dn, y, states, sums, convw, small, wide, spread, collapse, tri,
    d_gate, normed, weight,
):
    inner = heads * HEADDIM
    rows, width = proj.shape
    blocks = rows // BLOCK
    channels = inner + 2 * STATE
    last = blocks - 1

    def back(i):
        return jnp.maximum(last - i, 0)

    def late(i):
        return jnp.maximum(i - blocks, 0)

    return pl.pallas_call(
        partial(backward_kernel, heads, blocks),
        grid=(2 * blocks,),
        out_shape=[
            jax.ShapeDtypeStruct((rows, D), bf16),
            jax.ShapeDtypeStruct((channels + HEADS, D), bf16),
            jax.ShapeDtypeStruct((8, D), f32),
            jax.ShapeDtypeStruct((8, channels), f32),
            jax.ShapeDtypeStruct((8, LANES), f32),
            jax.ShapeDtypeStruct((8, inner), f32),
        ],
        in_specs=[
            SMEM, SMEM, SMEM,
            pl.BlockSpec((BLOCK, width), lambda i: (back(i), 0)),
            pl.BlockSpec((16, width), lambda i: (jnp.maximum((last - i) * (BLOCK // 16) - 1, 0), 0)),
            pl.BlockSpec((BLOCK, inner), lambda i: (back(i), 0)),
            pl.BlockSpec((BLOCK, inner), lambda i: (back(i), 0)),
            pl.BlockSpec((1, STATE, inner), lambda i: (back(i), 0, 0)),
            pl.BlockSpec((8, BLOCK), lambda i: (0, back(i))),
            whole(convw), whole(small), whole(wide), whole(spread), whole(collapse), whole(tri),
            pl.BlockSpec((BLOCK, inner), lambda i: (late(i), 0)),
            pl.BlockSpec((BLOCK, D), lambda i: (late(i), 0)),
            whole(weight),
        ],
        out_specs=[
            pl.BlockSpec((BLOCK, D), lambda i: (late(i), 0)),
            pl.BlockSpec((channels + HEADS, D), lambda i: (0, 0)),
            pl.BlockSpec((8, D), lambda i: (0, 0)),
            pl.BlockSpec((8, channels), lambda i: (0, 0)),
            pl.BlockSpec((8, LANES), lambda i: (0, 0)),
            pl.BlockSpec((8, inner), lambda i: (0, 0)),
        ],
        scratch_shapes=[
            pltpu.VMEM((rows * HALF, LANES), f32),
            pltpu.VMEM((BLOCK * HALF, LANES), f32),
            pltpu.VMEM((8, channels), f32),
            pltpu.VMEM((STATE, inner), f32),
            pltpu.VMEM((channels + LANES, D), f32),
        ],
        compiler_params=pltpu.CompilerParams(vmem_limit_bytes=VMEM_LIMIT),
        cost_estimate=pl.CostEstimate(flops=5 * rows * D * width, bytes_accessed=40_000_000, transcendentals=0),
        name="mixer_backward",
    )(
        me, ends, order, proj, proj, dn, y, states, sums, convw, small, wide, spread, collapse, tri,
        d_gate, normed, weight,
    )


def greet(axes, sizes, place):
    total = int(np.prod(sizes))
    barrier = pltpu.get_barrier_semaphore()

    def hail(d, carry):
        pl.semaphore_signal(
            barrier, inc=1, device_id=coordinates(axes, sizes, lax.rem(place + d, total)),
            device_id_type=pl.DeviceIdType.MESH,
        )
        return carry

    lax.fori_loop(1, total, hail, 0)
    pl.semaphore_wait(barrier, total - 1)


def coordinates(axes, sizes, place):
    where = {}
    for axis, size in reversed(list(zip(axes, sizes))):
        where[axis] = lax.rem(place, size)
        place = place // size
    return where


def my_place(axes, sizes):
    place = 0
    for axis, size in zip(axes, sizes):
        place = place * size + lax.axis_index(axis)
    return place


def share_kernel(axes, sizes, x, total, slots, send_sem, recv_sem):
    count = int(np.prod(sizes))
    me = my_place(axes, sizes)
    greet(axes, sizes, me)
    slots[me] = x[...]

    def copy_to(other, slot):
        return pltpu.make_async_remote_copy(
            src_ref=x, dst_ref=slots.at[slot], send_sem=send_sem.at[other], recv_sem=recv_sem.at[slot],
            device_id=coordinates(axes, sizes, other), device_id_type=pl.DeviceIdType.MESH,
        )

    def send(d, carry):
        copy_to(lax.rem(me + d, count), me).start()
        return carry

    def receive(d, carry):
        other = lax.rem(me + d, count)
        copy_to(other, other).wait_recv()
        return carry

    def sent(d, carry):
        copy_to(lax.rem(me + d, count), me).wait_send()
        return carry

    lax.fori_loop(1, count, send, 0)
    lax.fori_loop(1, count, receive, 0)
    lax.fori_loop(1, count, sent, 0)
    total[...] = lax.fori_loop(1, count, lambda i, acc: acc + slots[i], slots[0])


def share_sum(x, axes, sizes, collective_id):
    count = int(np.prod(sizes))
    return pl.pallas_call(
        partial(share_kernel, axes, sizes),
        out_shape=jax.ShapeDtypeStruct(x.shape, f32),
        in_specs=[pl.BlockSpec(memory_space=pltpu.VMEM)],
        out_specs=pl.BlockSpec(memory_space=pltpu.VMEM),
        scratch_shapes=[
            pltpu.VMEM((count,) + x.shape, f32),
            pltpu.SemaphoreType.DMA((count,)),
            pltpu.SemaphoreType.DMA((count,)),
        ],
        compiler_params=pltpu.CompilerParams(collective_id=collective_id, has_side_effects=True),
        name="share_sum",
    )(x)


def reduce_kernel(axes, sizes, x, total, slots, mine, send_sem, recv_sem, send_back, recv_back):
    count = int(np.prod(sizes))
    me = my_place(axes, sizes)
    greet(axes, sizes, me)
    slots[me] = x[me]

    def copy_to(other, slot):
        return pltpu.make_async_remote_copy(
            src_ref=x.at[other], dst_ref=slots.at[slot],
            send_sem=send_sem.at[other], recv_sem=recv_sem.at[slot],
            device_id=coordinates(axes, sizes, other), device_id_type=pl.DeviceIdType.MESH,
        )

    def copy_back(other, slot):
        return pltpu.make_async_remote_copy(
            src_ref=mine, dst_ref=total.at[slot],
            send_sem=send_back.at[other], recv_sem=recv_back.at[slot],
            device_id=coordinates(axes, sizes, other), device_id_type=pl.DeviceIdType.MESH,
        )

    def each(action):
        def one(d, carry):
            action(lax.rem(me + d, count))
            return carry

        lax.fori_loop(1, count, one, 0)

    each(lambda other: copy_to(other, me).start())
    each(lambda other: copy_to(other, other).wait_recv())
    mine[...] = lax.fori_loop(1, count, lambda i, acc: acc + slots[i], slots[0])
    total[me] = mine[...]
    each(lambda other: copy_back(other, me).start())
    each(lambda other: copy_to(other, me).wait_send())
    each(lambda other: copy_back(other, other).wait_recv())
    each(lambda other: copy_back(other, me).wait_send())


def reduce_sum(x, axes, sizes, collective_id):
    count = int(np.prod(sizes))
    return pl.pallas_call(
        partial(reduce_kernel, axes, sizes),
        out_shape=jax.ShapeDtypeStruct(x.shape, f32),
        in_specs=[pl.BlockSpec(memory_space=pltpu.VMEM)],
        out_specs=pl.BlockSpec(memory_space=pltpu.VMEM),
        scratch_shapes=[
            pltpu.VMEM(x.shape, f32),
            pltpu.VMEM(x.shape[1:], f32),
            pltpu.SemaphoreType.DMA((count,)),
            pltpu.SemaphoreType.DMA((count,)),
            pltpu.SemaphoreType.DMA((count,)),
            pltpu.SemaphoreType.DMA((count,)),
        ],
        compiler_params=pltpu.CompilerParams(collective_id=collective_id, has_side_effects=True),
        name="reduce_sum",
    )(x)


def assemble_kernel(group, heads, me, error, factor, *refs):
    gates, rests = refs[:group], refs[group : 2 * group]
    grad, merged, left = refs[2 * group :]
    inner = heads * HEADDIM
    turn = pl.program_id(0)
    exact_rows = 2 * STATE + HEADS

    for k in range(group):
        for piece, part in ((0, gates[k]), (1, rests[k])):

            @pl.when(turn == piece * group + (me[0] ^ k))
            def _():
                grad[...] = part[:inner, :].astype(f32)

    @pl.when(turn == 2 * group)
    def _():
        total = rests[0][inner:, :].astype(f32)
        for k in range(1, group):
            total = total + rests[k][inner:, :].astype(f32)
        grad[:exact_rows, :] = total
        grad[exact_rows:, :] = jnp.zeros((inner - exact_rows, grad.shape[1]), f32)

    sides = lax.broadcasted_iota(jnp.int32, (inner, 1), 0)
    known = sides < jnp.where(turn == 2 * group, exact_rows, inner)
    total = jnp.where(known, grad[...] + error[...], 0.0)
    merged[...] = total
    lanes = lax.broadcasted_iota(jnp.int32, factor.shape, 1)
    rows = jnp.where(lanes < jnp.where(turn == 2 * group, exact_rows, inner), factor[...], 0.0)
    part = lax.dot_general(
        rows, total, (((1,), (0,)), ((), ())), precision=highest, preferred_element_type=f32
    )
    left[...] = jnp.where(turn == 0, part, left[...] + part)


def assemble(heads, me, error, factor, gates, rests):
    group = len(gates)
    inner = heads * HEADDIM
    rows, columns = error.shape
    tall = pl.BlockSpec((inner, columns), lambda i: (i, 0))
    return pl.pallas_call(
        partial(assemble_kernel, group, heads),
        grid=(2 * group + 1,),
        out_shape=[jax.ShapeDtypeStruct((rows, columns), f32)] * 2
        + [jax.ShapeDtypeStruct((factor.shape[0], columns), f32)],
        in_specs=[SMEM, tall, pl.BlockSpec((factor.shape[0], inner), lambda i: (0, i))]
        + [whole(p) for p in gates + rests],
        out_specs=[tall] * 2 + [pl.BlockSpec((factor.shape[0], columns), lambda i: (0, 0))],
        compiler_params=pltpu.CompilerParams(vmem_limit_bytes=VMEM_LIMIT),
        name="assemble",
    )(me, error, factor, *gates, *rests)


def update_kernel(tall, flat, merged, moment, master, master_new, moment_new, error_new):
    approx = lax.dot_general(
        tall[...], flat[...], (((0,), (0,)), ((), ())), precision=highest, preferred_element_type=f32
    )
    fresh = momentum_decay * moment[...] + approx
    moment_new[...] = fresh
    master_new[...] = master[...] - weight_rate * fresh
    error_new[...] = merged[...] - approx


def update(tall, flat, merged, moment, master, step):
    rows, columns = merged.shape
    block = pl.BlockSpec((step, columns), lambda i: (i, 0))
    return pl.pallas_call(
        update_kernel,
        grid=(pl.cdiv(rows, step),),
        out_shape=[jax.ShapeDtypeStruct((rows, columns), f32)] * 3,
        in_specs=[pl.BlockSpec((tall.shape[0], step), lambda i: (0, i)), whole(flat)] + [block] * 3,
        out_specs=[block] * 3,
        compiler_params=pltpu.CompilerParams(vmem_limit_bytes=VMEM_LIMIT),
        name="update",
    )(tall, flat, merged, moment, master)


def split_vectors(vectors):
    widths = [D, CONV * XBC, XBC, HEADS, HEADS, HEADS, INNER]
    pieces = []
    offset = 0
    for span_size in widths:
        pieces.append(vectors[offset : offset + span_size])
        offset = offset + span_size
    norm_gain, conv_flat, conv_bias, dt_bias, decay_log, skip_gain, gate_gain = pieces
    return (
        norm_gain,
        conv_flat.reshape(CONV, XBC),
        conv_bias,
        dt_bias,
        decay_log,
        skip_gain,
        gate_gain,
    )


def spread_of(heads):
    lanes = np.arange(LANES)[:, None]
    return np.where(
        (lanes < 3 * heads) & (lanes % heads == np.arange(heads * HEADDIM)[None] // HEADDIM), 1.0, 0.0
    )


def collapse_of(heads):
    return np.where(np.arange(heads * HEADDIM)[:, None] // HEADDIM == np.arange(LANES)[None], 1.0, 0.0)


def local(
    tokens,
    cotangent,
    order,
    lengths,
    vectors,
    vector_moment,
    in_master,
    in_moment,
    in_error,
    in_factor,
    out_master,
    out_moment,
    out_error,
    out_factor,
):
    replicas = lax.axis_size("rep")
    group = lax.axis_size("grp")
    me = lax.axis_index("grp")
    heads = HEADS // group
    inner = INNER // group
    keys = 2 * STATE

    norm_gain, conv_weight, conv_bias, dt_bias, decay_log, skip_gain, gate_gain = split_vectors(vectors)

    def swap(x, k):
        return lax.ppermute(x, "grp", [(i, i ^ k) for i in range(group)])

    in_master, in_moment, in_error = in_master.T, in_moment.T, in_error[0].T
    in_factor, out_factor = in_factor.T, out_factor.T
    in_cols = in_master.shape[1]

    in16 = in_master.astype(bf16)

    stream = tokens[0].astype(f32)
    inv_rms = lax.rsqrt(jnp.mean(stream * stream, axis=-1, keepdims=True) + epsilon)
    normed_own = (stream * inv_rms * norm_gain).astype(bf16)
    normed_parts = [normed_own] + [swap(normed_own, k) for k in range(1, group)]
    normed = jnp.concatenate(normed_parts, axis=0)
    cot_own, normed = lax.optimization_barrier((cotangent[0], normed))
    cot_all = jnp.concatenate([cot_own] + [swap(cot_own, k) for k in range(1, group)], axis=0)
    positions = order.shape[1]
    rows = positions // group
    slots = ((order // rows) ^ me) * rows + order % rows
    place = jnp.reshape(me, (1,)).astype(jnp.int32)

    ends = jnp.cumsum(lengths[0]).astype(jnp.int32)

    def own(a, size):
        return lax.dynamic_slice_in_dim(a, me * size, size, axis=a.ndim - 1)

    conv_all = jnp.concatenate([conv_weight, conv_bias[None]], axis=0)
    convw = jnp.concatenate([own(conv_all[:, :INNER], inner), conv_all[:, INNER:]], axis=1)
    convw = jnp.pad(convw, ((0, 8 - CONV - 1), (0, 0)))
    small = jnp.stack([own(dt_bias, heads), own(jnp.exp(decay_log), heads)])
    small = jnp.pad(small, ((0, 6), (0, LANES - heads)))
    own_gain = own(gate_gain, inner)
    wide = jnp.stack([jnp.repeat(own(skip_gain, heads), HEADDIM), own_gain])
    wide = jnp.pad(wide, ((0, 6), (0, 0)))
    spread = jnp.asarray(spread_of(heads), bf16)
    collapse = jnp.asarray(collapse_of(heads), bf16)
    tri = jnp.asarray(np.tril(np.ones((BLOCK, BLOCK))), bf16)

    out16 = out_master.astype(bf16)
    weight, normed, cot_all, proj, y, states, dn, sums = front_call(
        heads, ends, slots, normed_own, cotangent[0], in16, out16, convw, small, wide, spread, tri
    )
    sums8 = jnp.pad(jnp.stack([sums[0], sums[8]]), ((0, 6), (0, 0)))
    result_part, d_gate, out_owned, in_gate, d_gain = gate_call(
        heads, slots, proj, y, dn, sums8, wide, cot_all, normed, out16
    )

    def to_owners(a):
        pieces = [lax.dynamic_slice_in_dim(a, (me ^ k) * in_cols, in_cols, axis=1) for k in range(group)]
        return pieces[:1] + [swap(pieces[k], k) for k in range(1, group)]

    gates = to_owners(in_gate.astype(bf16))
    result_part = result_part.reshape(group, rows, D)
    result = stream + result_part[0].astype(f32)
    for k in range(1, group):
        result = result + swap(result_part[k], k).astype(f32)
    mixed_rows = result.astype(bf16)[None]

    d_normed_part, in_rest, d_norm_gain, d_conv, d_small, d_skip = backward_call(
        heads, place, ends, slots, proj, dn, y, states, sums8, convw, small, wide, spread, collapse, tri,
        d_gate, normed, weight,
    )
    rests = to_owners(in_rest)
    in_owned, in_merged, in_left = assemble(heads, place, in_error, in_factor, gates, rests)
    d_norm_gain = d_norm_gain[0] / norm_gain
    d_normed_part, in_owned = lax.optimization_barrier((d_normed_part, in_owned))
    d_normed_part = d_normed_part.reshape(group, rows, D)
    d_normed = d_normed_part[0].astype(f32)
    for k in range(1, group):
        d_normed = d_normed + swap(d_normed_part[k], k).astype(f32)
    scaled = d_normed * norm_gain
    lean = jnp.mean(scaled * stream, axis=-1, keepdims=True)
    d_stream = inv_rms * scaled - stream * (inv_rms * inv_rms * inv_rms * lean)
    input_rows = (cotangent[0].astype(f32) + d_stream).astype(bf16)[None]

    def placed(a, total):
        size = a.shape[-1]
        zero = jnp.zeros(a.shape[:-1] + (total,), f32)
        return lax.dynamic_update_slice_in_dim(zero, a, me * size, axis=a.ndim - 1)

    d_conv_all = jnp.concatenate([placed(d_conv[:5, :inner], INNER), d_conv[:5, inner:]], axis=1)
    d_skip = jnp.sum(d_skip[0].reshape(heads, HEADDIM), axis=1)
    vector_local = jnp.concatenate(
        [
            d_norm_gain,
            d_conv_all[:CONV].reshape(-1),
            d_conv_all[CONV],
            placed(d_small[0, :heads], HEADS),
            placed(d_small[1, :heads], HEADS),
            placed(d_skip, HEADS),
            placed(d_gain[0], INNER),
        ]
    )

    out_merged = out_owned + out_error[0]

    def exact(a, b, dims):
        return lax.dot_general(a, b, (dims, ((), ())), precision=highest, preferred_element_type=f32)

    left = jnp.concatenate([in_left, exact(out_factor, out_merged, ((1,), (1,)))], axis=1)
    left = share_sum(left, ("rep",), (replicas,), 1)
    in_left, out_left = left[:, :in_cols], left[:, in_cols:]
    rank = left.shape[0]
    grams = jnp.concatenate([exact(in_left, in_left, ((1,), (1,))), exact(out_left, out_left, ((1,), (1,)))], axis=1)
    bundle = [
        exact(in_left, in_merged, ((1,), (1,))),
        exact(out_left, out_merged, ((1,), (0,))),
        grams,
        jnp.pad(vector_local, (0, -vector_local.size % rank)).reshape(rank, -1),
    ]
    bundle = [jnp.pad(b, ((0, 0), (0, -b.shape[1] % LANES))) for b in bundle]
    edges = np.cumsum([0] + [b.shape[1] for b in bundle])
    devices = group * replicas
    share = -(-int(edges[-1]) // (devices * LANES)) * LANES
    packed = jnp.pad(jnp.concatenate(bundle, axis=1), ((0, 0), (0, devices * share - int(edges[-1]))))
    packed = jnp.swapaxes(packed.reshape(rank, devices, share), 0, 1)
    packed = reduce_sum(packed, ("grp", "rep"), (group, replicas), 2)
    packed = jnp.swapaxes(packed, 0, 1).reshape(rank, devices * share)
    in_right, out_right, grams, vector_sum = [
        packed[:, edges[i] : edges[i + 1]] for i in range(4)
    ]
    columns = -(-vectors.shape[0] // rank)
    vector_grad = vector_sum[:, :columns].reshape(-1)[: vectors.shape[0]] / replicas

    def settle(gram, left_t, right_t):
        inverse = lax.linalg.triangular_solve(
            jnp.linalg.cholesky(gram / replicas), jnp.eye(rank, dtype=f32), left_side=True, lower=True
        )
        return exact(inverse, left_t, ((1,), (0,))), exact(inverse, right_t, ((1,), (0,))) / replicas

    in_basis, in_right = settle(grams[:, :rank], in_left, in_right[:, : in_master.shape[0]])
    out_basis, out_right = settle(grams[:, rank : 2 * rank], out_left, out_right[:, : out_master.shape[1]])
    in_new, in_moment_new, in_error_new = update(
        in_right, in_basis, in_merged, in_moment, in_master, inner
    )
    out_new, out_moment_new, out_error_new = update(
        out_basis, out_right, out_merged, out_moment, out_master, LANES
    )
    vector_moment_new = momentum_decay * vector_moment + vector_grad
    vector_new = vectors - vector_rate * vector_moment_new
    return (
        mixed_rows,
        input_rows,
        in_owned.T[None],
        out_owned[None],
        vector_grad,
        in_new.T,
        in_moment_new.T,
        in_error_new.T[None],
        in_right.T,
        out_new,
        out_moment_new,
        out_error_new[None],
        out_right.T,
        vector_new,
        vector_moment_new,
    )


def solution(mesh):
    placed = (
        P("rep", "grp", None),
        P("rep", "grp", None),
        P("rep", None),
        P("rep", None),
        P(),
        P(),
        P("grp", None),
        P("grp", None),
        P("rep", "grp", None),
        P(),
        P("grp", None),
        P("grp", None),
        P("rep", "grp", None),
        P(),
    )
    return jax.shard_map(
        local,
        mesh=mesh,
        in_specs=placed,
        out_specs=(
            P("rep", "grp", None),
            P("rep", "grp", None),
            P("rep", "grp", None),
            P("rep", "grp", None),
            P(),
            P("grp", None),
            P("grp", None),
            P("rep", "grp", None),
            P(),
            P("grp", None),
            P("grp", None),
            P("rep", "grp", None),
            P(),
            P(),
            P(),
        ),
        check_vma=False,
    )
```

```python
from functools import partial
import jax
import jax.numpy as jnp
import numpy as np
from jax import lax
from jax.experimental import pallas as pl
from jax.experimental.pallas import tpu as pltpu
from jax.sharding import PartitionSpec as P
D = 1024
HEADS = 32
HEADDIM = 64
STATE = 128
CONV = 4
BLOCK = 256
INNER = 2048
XBC = 2304
LANES = 128
REACH = CONV - 1
epsilon = 1e-05
momentum_decay = 0.9
weight_rate = 0.001
vector_rate = 0.02
highest = lax.Precision.HIGHEST
f32 = jnp.float32
bf16 = jnp.bfloat16
LOG2E = float(np.log2(np.e))


def nn(a, b):
    return lax.dot_general(a, b, (((1,), (0,)), ((), ())), preferred_element_type=f32)


def nt(a, b):
    return lax.dot_general(a, b, (((1,), (1,)), ((), ())), preferred_element_type=f32)


def tn(a, b):
    return lax.dot_general(a, b, (((0,), (0,)), ((), ())), preferred_element_type=f32)


def sigmoid(x):
    return 0.5 * jnp.tanh(0.5 * x) + 0.5


def pack3(x, width):
    hi = x.astype(bf16).astype(f32)
    rest = x - hi
    mid = rest.astype(bf16).astype(f32)
    low = rest - mid
    return (hi + pltpu.roll(mid, width, 1) + pltpu.roll(low, 2 * width, 1)).astype(bf16)


def unpack3(x, width):
    return x + pltpu.roll(x, LANES - width, 1) + pltpu.roll(x, LANES - 2 * width, 1)


def block_parts(heads, place, ends, x_ext, dt_raw, convw, small, wide, spread, tri):
    inner = heads * HEADDIM
    first = place * BLOCK
    column = first + lax.broadcasted_iota(jnp.int32, (BLOCK, 1), 0)
    row = first + lax.broadcasted_iota(jnp.int32, (1, BLOCK), 1)

    def segment(pos):
        total = jnp.zeros_like(pos)
        for k in range(ends.shape[0]):
            total = total + (ends[k] <= pos).astype(jnp.int32)
        return jnp.where(pos >= 0, total, -1)

    seg = segment(column)
    reach = [None] + [(segment(column - d) == seg).astype(f32) for d in range(1, CONV)]
    acc = convw[CONV : CONV + 1] + convw[REACH : REACH + 1] * x_ext[8:]
    for d in range(1, CONV):
        acc = acc + convw[REACH - d : CONV - d] * (x_ext[8 - d : 8 - d + BLOCK] * reach[d])
    sig = sigmoid(acc)
    mixed = (acc * sig).astype(bf16)
    values = mixed[:, :inner].astype(f32)
    write_keys = mixed[:, inner : inner + STATE]
    read_keys = mixed[:, inner + STATE :]

    lane = lax.broadcasted_iota(jnp.int32, (BLOCK, LANES), 1)
    live = lane < heads
    shifted = dt_raw + small[0:1]
    step = jnp.where(live, jnp.maximum(shifted, 0.0) + jnp.log1p(jnp.exp(-jnp.abs(shifted))), 0.0)
    log_decay = -small[1:2] * step
    cum = jnp.where(live, unpack3(nn(tri, pack3(log_decay, heads)), heads), 0.0) * LOG2E
    cum_rows = jnp.transpose(cum)
    enters = (seg == segment(column * 0 + (first - 1))).astype(f32)
    leaves = (seg == segment(column * 0 + (first + BLOCK - 1))).astype(f32)
    carry = jnp.where(live, jnp.exp2(cum) * enters, 0.0)
    tail = jnp.where(live, jnp.exp2(cum[BLOCK - 1 :] - cum) * leaves, 0.0)

    def expand(x):
        return nn(pack3(x, heads), spread)

    step_wide, carry_wide, tail_wide = expand(step), expand(carry), expand(tail)
    scaled = values * step_wide
    same = (seg == segment(row)) & (column >= row)
    hidden = jnp.where(same, 0.0, -1e30)
    read_write = nt(read_keys, write_keys)
    return dict(
        acc=acc, sig=sig, values=values, write_keys=write_keys, read_keys=read_keys, live=live,
        shifted=shifted, step=step, log_decay=log_decay, cum=cum, cum_rows=cum_rows,
        carry_wide=carry_wide, tail_wide=tail_wide, step_wide=step_wide, scaled=scaled,
        hidden=hidden, read_write=read_write, reach=reach, segment=segment, column=column, seg=seg,
    )


def decay_of(part, h):
    return jnp.exp2(part["cum"][:, h : h + 1] - part["cum_rows"][h : h + 1, :] + part["hidden"])
PITCH = 16
PAD = 16
HALF = 8
VMEM_LIMIT = 56 * 1024 * 1024


def store_rows(ref, base, value, pitch):
    count = value.shape[0]
    for c in range(value.shape[1] // LANES):
        ref[pl.ds(base * pitch + c, count, stride=pitch), :] = value[:, c * LANES : (c + 1) * LANES]


def load_rows(ref, base, count, chunks, pitch):
    return jnp.concatenate(
        [ref[pl.ds(base * pitch + c, count, stride=pitch), :] for c in range(chunks)], axis=1
    )


def gather_rows(order, first, source, target, pitch):
    def some(i, carry):
        for u in range(8):
            row = order[0, first + i * 8 + u] * pitch
            target[pl.ds(pl.multiple_of((i * 8 + u) * pitch, pitch), pitch), :] = source[pl.ds(row, pitch), :]
        return carry

    lax.fori_loop(0, BLOCK // 8, some, 0)


def row_sums(total):
    hi = total.astype(bf16)
    low = (total - hi.astype(f32)).astype(bf16)
    ones = jnp.ones((8, LANES), bf16)
    return nt(ones, hi) + nt(ones, low)


def fold(value):
    total = value[:, :LANES]
    for c in range(1, value.shape[1] // LANES):
        total = total + value[:, c * LANES : (c + 1) * LANES]
    return total


def whole(a):
    return pl.BlockSpec(a.shape, lambda i: (0,) * a.ndim)
SMEM = pl.BlockSpec(memory_space=pltpu.SMEM)


def front_kernel(
    heads, rows, ends, order, tokens, cotangent, master, out16, convw, small, wide, spread, tri,
    weight_out, normed_out, cot_out, proj_out, y_out, states_out, dn_out, sums_out,
    weight, normed, cot, given, packed, proj, y, states, dn, halo, state, sums, arrived,
    send, recv, keep, save,
):
    group = order.shape[1] // rows
    inner = heads * HEADDIM
    shared = 2 * inner + 2 * STATE
    positions = order.shape[1]
    blocks = positions // BLOCK
    in_cols = master.shape[1]
    me = lax.axis_index("grp")
    rep = lax.axis_index("rep")
    core = lax.rem(rep, 2)
    sibling = {"rep": rep + 1 - 2 * core}
    mesh_id = pl.DeviceIdType.MESH
    lane = lax.broadcasted_iota(jnp.int32, (BLOCK, LANES), 1)
    half = rows // 2

    barrier = pltpu.get_barrier_semaphore()
    for k in range(1, group):
        pl.semaphore_signal(barrier, inc=1, device_id={"grp": me ^ k}, device_id_type=mesh_id)
    pl.semaphore_signal(barrier, inc=1, device_id=sibling, device_id_type=mesh_id)

    pieces = [(0, 0, inner), (INNER, inner, inner), (2 * INNER, 2 * inner, 2 * STATE), (2 * INNER + 2 * STATE, shared, HEADS)]

    def remote(src, dst, index, target):
        return pltpu.make_async_remote_copy(
            src_ref=src, dst_ref=dst, send_sem=send.at[index], recv_sem=recv.at[index],
            device_id=target, device_id_type=mesh_id,
        )

    def columns(owner):
        return pl.ds(pl.multiple_of(owner * in_cols, in_cols), in_cols)

    def weight_copy(k, p, owner, reader):
        source, target, count = pieces[p]
        part = count // 2
        start = source + core * part + (reader * count if p < 2 else 0)
        return remote(
            master.at[pl.ds(pl.multiple_of(start, 16), part), :],
            weight.at[pl.ds(pl.multiple_of(target + core * part, 16), part), columns(owner)],
            4 * (k - 1) + p, {"grp": me ^ k},
        )

    def twin_copy(k, p, side):
        target, part = pieces[p][1], pieces[p][2] // 2
        where = weight.at[pl.ds(pl.multiple_of(target + side * part, 16), part), columns(me ^ k)]
        return remote(where, where, 12 + 4 * (k - 1) + p, sibling)

    def slot(ref, k, part=None):
        if part is None:
            return ref.at[pl.ds(k * rows, rows), :]
        return ref.at[pl.ds(k * rows + part * half, half), :]

    def row_copy(own, ref, k, base):
        return remote(own, slot(ref, k), base + k - 1, {"grp": me ^ k})

    def pass_copy(ref, k, base):
        return remote(slot(ref, k, k - 1), slot(ref, 3, k - 1), base + 1 + k, {"grp": me ^ (3 - k)})

    own = []
    for p in range(4):
        source, target, count = pieces[p]
        start = source + (me * count if p < 2 else 0)
        own.append(
            pltpu.make_async_copy(
                master.at[pl.ds(pl.multiple_of(start, 16), count), :],
                weight.at[pl.ds(target, count), columns(me)], keep.at[p],
            )
        )
    own.append(pltpu.make_async_copy(tokens, slot(normed, 0), keep.at[4]))
    own.append(pltpu.make_async_copy(cotangent, slot(cot, 0), keep.at[5]))
    for c in own:
        c.start()

    pl.semaphore_wait(barrier, group)
    for k in (1, 2, 3):
        for p in range(4):
            weight_copy(k, p, me, me ^ k).start()
    for k in (1, 2):
        row_copy(tokens, normed, k, 24).start()
    for k in (1, 2, 3):
        for p in range(4):
            weight_copy(k, p, me ^ k, me).wait_recv()
            twin_copy(k, p, core).start()
    for c in own:
        c.wait()
    for k in (1, 2, 3):
        for p in range(4):
            twin_copy(k, p, 1 - core).wait_recv()

    def project(k):
        def one(i, carry):
            first = pl.multiple_of(k * rows + i * BLOCK, BLOCK)
            x = normed[pl.ds(first, BLOCK), :]
            main = nt(x, weight[:shared, :]).astype(bf16).astype(f32)
            rates = nt(x, weight[shared:, :]).astype(bf16).astype(f32)
            rates = jnp.concatenate([rates, jnp.zeros((BLOCK, LANES - HEADS), f32)], axis=1)
            rates = pltpu.roll(rates, lax.rem(LANES - me * heads, LANES), 1)
            rates = jnp.where(lane < heads, rates, 0.0)
            store_rows(given, first, jnp.concatenate([main, rates], axis=1), PITCH)
            return carry

        lax.fori_loop(0, rows // BLOCK, one, 0)

    project(0)
    for k in (1, 2):
        row_copy(tokens, normed, k, 24).wait_recv()
        pass_copy(normed, k, 24).start()
    for k in (1, 2):
        row_copy(cotangent, cot, k, 28).start()
    project(1)
    project(2)
    for k in (1, 2):
        pass_copy(normed, k, 24).wait_recv()
    project(3)

    weight_save = pltpu.make_async_copy(weight, weight_out, save.at[0])
    normed_save = pltpu.make_async_copy(normed, normed_out, save.at[1])
    weight_save.start()
    normed_save.start()
    halo[...] = jnp.zeros_like(halo)
    state[...] = jnp.zeros_like(state)

    def scan(place, carry):
        @pl.when(place == blocks - 2)
        def _():
            for k in (1, 2):
                row_copy(cotangent, cot, k, 28).wait_recv()
                pass_copy(cot, k, 28).start()

        base = pl.multiple_of(place * BLOCK, BLOCK)
        gather_rows(order, base, given, packed, PITCH)
        x_all = load_rows(packed, 0, BLOCK, shared // LANES + 1, PITCH)
        proj[pl.ds(base, BLOCK), :] = x_all.astype(bf16)
        gate_all = x_all[:, :inner]
        x = x_all[:, inner:shared]
        x_ext = jnp.concatenate([halo[...], x], axis=0)
        halo[...] = x[BLOCK - 8 :]
        part = block_parts(
            heads, place, ends, x_ext, x_all[:, shared:], convw[...], small[...], wide[...], spread[...], tri[...]
        )
        states[place] = state[...]
        scaled = part["scaled"].astype(bf16)
        carried = part["carry_wide"] * nn(part["read_keys"], state[...].astype(bf16))
        total = None
        for pair in range(heads // 2):
            cols = slice(pair * LANES, (pair + 1) * LANES)
            halves = []
            for h in (2 * pair, 2 * pair + 1):
                tile = (decay_of(part, h) * part["read_write"]).astype(bf16)
                halves.append(nn(tile, scaled[:, cols]))
            local = jnp.where(lane < HEADDIM, halves[0], halves[1])
            out = local + carried[:, cols] + wide[0:1, cols] * part["values"][:, cols]
            y[pl.ds(base, BLOCK), cols] = out
            gate = gate_all[:, cols]
            gated = out * (gate * sigmoid(gate))
            total = gated * gated if total is None else total + gated * gated
        sums[0:8, pl.ds(base, BLOCK)] = row_sums(total)
        leaving = (part["tail_wide"] * part["scaled"]).astype(bf16)
        state[...] = part["carry_wide"][BLOCK - 1 :] * state[...] + tn(part["write_keys"], leaving)
        return carry

    lax.fori_loop(0, blocks, scan, 0)
    saves = [
        pltpu.make_async_copy(proj, proj_out, save.at[2]),
        pltpu.make_async_copy(y, y_out, save.at[3]),
        pltpu.make_async_copy(states, states_out, save.at[4]),
    ]
    for c in saves:
        c.start()

    def pull(k):
        def one(i, carry):
            first = pl.multiple_of(k * rows + i * BLOCK, BLOCK)
            store_rows(given, first, nt(cot[pl.ds(first, BLOCK), :], out16[...]), HALF)
            return carry

        lax.fori_loop(0, rows // BLOCK, one, 0)

    for k in range(3):
        pull(k)
    for k in (1, 2):
        pass_copy(cot, k, 28).wait_recv()
    pull(3)
    cot_save = pltpu.make_async_copy(cot, cot_out, save.at[5])
    cot_save.start()

    def lean(place, carry):
        base = pl.multiple_of(place * BLOCK, BLOCK)
        gather_rows(order, base, given, packed, HALF)
        grad = load_rows(packed, 0, BLOCK, inner // LANES, HALF)
        dn[pl.ds(base, BLOCK), :] = grad.astype(bf16)
        x = proj[pl.ds(base, BLOCK), :inner].astype(f32)
        gated = y[pl.ds(base, BLOCK), :] * (x * sigmoid(x))
        sums[8:16, pl.ds(base, BLOCK)] = row_sums(fold(grad * wide[1:2] * gated))
        return carry

    lax.fori_loop(0, blocks, lean, 0)
    dn_save = pltpu.make_async_copy(dn, dn_out, save.at[6])
    dn_save.start()

    def sums_copy(k):
        return remote(sums, arrived.at[k - 1], 31 + k, {"grp": me ^ k})

    for k in (1, 2, 3):
        sums_copy(k).start()
    for k in (1, 2, 3):
        sums_copy(k).wait_recv()
    sums_out[0:8, :] = sums[0:8, :] + arrived[0, 0:8, :] + arrived[1, 0:8, :] + arrived[2, 0:8, :]
    sums_out[8:16, :] = sums[8:16, :] + arrived[0, 8:16, :] + arrived[1, 8:16, :] + arrived[2, 8:16, :]

    for k in (1, 2, 3):
        sums_copy(k).wait_send()
        for p in range(4):
            weight_copy(k, p, me, me ^ k).wait_send()
            twin_copy(k, p, core).wait_send()
    for k in (1, 2):
        row_copy(tokens, normed, k, 24).wait_send()
        pass_copy(normed, k, 24).wait_send()
        row_copy(cotangent, cot, k, 28).wait_send()
        pass_copy(cot, k, 28).wait_send()
    for c in [weight_save, normed_save, cot_save, dn_save] + saves:
        c.wait()
VM = pl.BlockSpec(memory_space=pltpu.VMEM)
ANY = pl.BlockSpec(memory_space=pl.ANY)


def front_call(heads, ends, order, tokens, cotangent, master, out16, convw, small, wide, spread, tri):
    inner = heads * HEADDIM
    rows = tokens.shape[0]
    positions = order.shape[1]
    width = 2 * inner + 2 * STATE + LANES
    blocks = positions // BLOCK
    channels = inner + 2 * STATE
    weight = (2 * inner + 2 * STATE + HEADS, D)
    return pl.pallas_call(
        partial(front_kernel, heads, rows),
        out_shape=[
            jax.ShapeDtypeStruct(weight, bf16),
            jax.ShapeDtypeStruct((positions, D), bf16),
            jax.ShapeDtypeStruct((positions, D), bf16),
            jax.ShapeDtypeStruct((positions, width), bf16),
            jax.ShapeDtypeStruct((positions, inner), f32),
            jax.ShapeDtypeStruct((blocks, STATE, inner), f32),
            jax.ShapeDtypeStruct((positions, inner), bf16),
            jax.ShapeDtypeStruct((16, positions), f32),
        ],
        in_specs=[SMEM, SMEM, ANY, ANY, ANY] + [VM] * 6,
        out_specs=[ANY] * 7 + [VM],
        scratch_shapes=[
            pltpu.VMEM(weight, bf16),
            pltpu.VMEM((positions, D), bf16),
            pltpu.VMEM((positions, D), bf16),
            pltpu.VMEM((positions * PITCH, LANES), f32),
            pltpu.VMEM((BLOCK * PITCH, LANES), f32),
            pltpu.VMEM((positions, width), bf16),
            pltpu.VMEM((positions, inner), f32),
            pltpu.VMEM((blocks, STATE, inner), f32),
            pltpu.VMEM((positions, inner), bf16),
            pltpu.VMEM((8, channels), f32),
            pltpu.VMEM((STATE, inner), f32),
            pltpu.VMEM((16, positions), f32),
            pltpu.VMEM((3, 16, positions), f32),
            pltpu.SemaphoreType.DMA((35,)),
            pltpu.SemaphoreType.DMA((35,)),
            pltpu.SemaphoreType.DMA((6,)),
            pltpu.SemaphoreType.DMA((7,)),
        ],
        compiler_params=pltpu.CompilerParams(
            vmem_limit_bytes=60 * 1024 * 1024, collective_id=3, has_side_effects=True
        ),
        name="front",
    )(ends, order, tokens, cotangent, master, out16, convw, small, wide, spread, tri)


def norm_parts(sums):
    columns = jnp.transpose(sums)
    scale = lax.rsqrt(columns[:, 0:1] * (1.0 / INNER) + epsilon)
    return scale, scale * scale * scale * columns[:, 1:2] * (1.0 / INNER)


def backward_block(
    heads, me, place, ends, proj, dn, y, states, sums, convw, small, wide, spread, collapse, tri,
    d_conv, d_small, d_skip, moved, after, d_state,
):
    inner = heads * HEADDIM

    base = pl.multiple_of(place * BLOCK, BLOCK)
    here = pl.ds(base, BLOCK)
    after_pad = pl.ds(pl.multiple_of(place * BLOCK + PAD, PAD), BLOCK)
    x = proj[after_pad, inner : 2 * inner + 2 * STATE].astype(f32)
    prior = proj[pl.ds(base, PAD), inner : 2 * inner + 2 * STATE].astype(f32)[PAD - 8 :]
    x_ext = jnp.concatenate([prior, x], axis=0)
    dt_raw = proj[after_pad, 2 * inner + 2 * STATE :].astype(f32)
    part = block_parts(
        heads, place, ends, x_ext, dt_raw, convw[...], small[...], wide[...], spread[...], tri[...]
    )
    values, scaled32 = part["values"], part["scaled"]
    read_keys, write_keys = part["read_keys"], part["write_keys"]
    carry_wide, tail_wide, step_wide = part["carry_wide"], part["tail_wide"], part["step_wide"]
    skip, gain = wide[0:1], wide[1:2]

    scale, pull = norm_parts(sums[:, here])
    gate = proj[after_pad, :inner].astype(f32)
    gate_sig = sigmoid(gate)
    silu = gate * gate_sig
    out = y[here, :]
    gated = out * silu
    grad = dn[here, :].astype(f32)
    d_gated = scale * (grad * gain) - gated * pull
    d_out = d_gated * silu
    state = states[place]
    d_leaving = d_state[...]
    d_leaving16 = d_leaving.astype(bf16)
    d_out16 = d_out.astype(bf16)
    scaled = scaled32.astype(bf16)
    d_carried = (carry_wide * d_out).astype(bf16)
    d_tail = tail_wide * nn(write_keys, d_leaving16)
    leaving = (tail_wide * scaled32).astype(bf16)
    d_write = nt(leaving, d_leaving16)
    d_read = nt(d_carried, state.astype(bf16))
    carry_last = carry_wide[BLOCK - 1 :]
    d_state[...] = carry_last * d_leaving + tn(read_keys, d_carried)

    lane = lax.broadcasted_iota(jnp.int32, (BLOCK, LANES), 1)
    d_rw = None
    pieces = []
    for pair in range(heads // 2):
        cols = slice(pair * LANES, (pair + 1) * LANES)
        halves = []
        for k, h in enumerate((2 * pair, 2 * pair + 1)):
            own = (lane < HEADDIM) if k == 0 else (lane >= HEADDIM)
            decay = decay_of(part, h)
            tile = (decay * part["read_write"]).astype(bf16)
            mine = jnp.where(own, d_out16[:, cols], jnp.zeros((), bf16))
            d_tile = nt(mine, scaled[:, cols]) * decay
            d_rw = d_tile if d_rw is None else d_rw + d_tile
            halves.append(tn(tile, d_out16[:, cols]))
        pieces.append(jnp.where(lane < HEADDIM, halves[0], halves[1]))
    d_scaled = jnp.concatenate(pieces, axis=1) + d_tail
    d_rw16 = d_rw.astype(bf16)
    d_read = d_read + nn(d_rw16, write_keys)
    d_write = d_write + tn(d_rw16, read_keys)

    def gather_heads(v):
        hi = v.astype(bf16)
        low = (v - hi.astype(f32)).astype(bf16)
        return nn(hi, collapse[...]) + nn(low, collapse[...])

    flow = d_out * (out - skip * values) - scaled32 * d_scaled
    last_flow = jnp.sum(scaled32 * d_tail, axis=0, keepdims=True) + carry_last * jnp.sum(
        d_leaving * state, axis=0, keepdims=True
    )
    rows = lax.broadcasted_iota(jnp.int32, (BLOCK, 1), 0)
    flow = flow + jnp.where(rows == BLOCK - 1, last_flow, 0.0)
    d_cum = gather_heads(flow)
    d_log = unpack3(tn(tri[...], pack3(d_cum, heads)), heads)
    d_log = jnp.where(part["live"], d_log, 0.0)
    d_step = gather_heads(d_scaled * values) - small[1:2] * d_log
    d_dt = jnp.where(part["live"], d_step * sigmoid(part["shifted"]), 0.0)
    d_small[0:1, :] += jnp.sum(d_dt, axis=0, keepdims=True)
    d_small[1:2, :] += jnp.sum(d_log * part["log_decay"], axis=0, keepdims=True)
    d_skip[0:1, :] += jnp.sum(d_out * values, axis=0, keepdims=True)

    d_values = d_scaled * step_wide + skip * d_out
    acc, sig = part["acc"], part["sig"]
    d_acc = jnp.concatenate([d_values, d_write, d_read], axis=1) * (
        sig * (1.0 + acc * (1.0 - sig))
    )
    d_ext = jnp.concatenate([d_acc, after[...]], axis=0)
    after[...] = d_acc[:8]
    d_x = convw[REACH : REACH + 1] * d_acc
    d_conv[REACH : REACH + 1, :] += jnp.sum(d_acc * x, axis=0, keepdims=True)
    d_conv[CONV : CONV + 1, :] += jnp.sum(d_acc, axis=0, keepdims=True)
    for d in range(1, CONV):
        ahead = (part["segment"](part["column"] + d) == part["seg"]).astype(f32)
        d_x = d_x + convw[REACH - d : CONV - d] * (d_ext[d : d + BLOCK] * ahead)
        d_conv[REACH - d : CONV - d, :] += jnp.sum(
            d_acc * (x_ext[8 - d : 8 - d + BLOCK] * part["reach"][d]), axis=0, keepdims=True
        )
    d_rates = pltpu.roll(d_dt, me * heads, 1)
    d_all = jnp.concatenate([d_x, d_rates], axis=1).astype(bf16).astype(f32)
    store_rows(moved, base, d_all, HALF)


def back_kernel(
    heads, rows, ends, inverse, proj_in, y_in, states_in, dn_in, normed_in, cot_in, weight_in, sums, out16,
    convw, small, wide, spread, collapse, tri,
    own_result, results, gates, rests, back0, back1, back2, back3,
    out_grad, d_norm_gain, d_gain, d_conv, d_small, d_skip,
    proj, y, states, dn, normed, cot, weight, moved, packed, partials, d_gate, gate16, total, rest16,
    after, d_state, load, save, send, recv,
):
    inner = heads * HEADDIM
    shared = 2 * inner + 2 * STATE
    channels = shared - inner
    positions = inverse.shape[1]
    group = positions // rows
    blocks = positions // BLOCK
    per = rows // BLOCK
    in_cols = gates.shape[2]
    me = lax.axis_index("grp")
    mesh_id = pl.DeviceIdType.MESH
    outs = (back0, back1, back2, back3)

    barrier = pltpu.get_barrier_semaphore()
    for k in range(1, group):
        pl.semaphore_signal(barrier, inc=1, device_id={"grp": me ^ k}, device_id_type=mesh_id)

    proj_rows = proj.at[pl.ds(PAD, positions), :]
    loads = [
        pltpu.make_async_copy(src, dst, load.at[i])
        for i, (src, dst) in enumerate(
            [
                (proj_in, proj_rows), (y_in, y), (dn_in, dn), (cot_in, cot), (normed_in, normed),
                (states_in, states), (weight_in, weight),
            ]
        )
    ]
    for c in loads:
        c.start()
    proj[0:PAD, :] = jnp.zeros((PAD, proj.shape[1]), bf16)
    after[...] = jnp.zeros_like(after)
    d_state[...] = jnp.zeros_like(d_state)
    d_conv[...] = jnp.zeros_like(d_conv)
    d_small[...] = jnp.zeros_like(d_small)
    d_skip[...] = jnp.zeros_like(d_skip)
    d_gain[...] = jnp.zeros_like(d_gain)
    d_norm_gain[...] = jnp.zeros_like(d_norm_gain)
    total[...] = jnp.zeros_like(total)
    out_grad[...] = jnp.zeros_like(out_grad)
    pl.semaphore_wait(barrier, group - 1)
    for c in loads[:3]:
        c.wait()

    def remote(src, dst, index, k):
        return pltpu.make_async_remote_copy(
            src_ref=src, dst_ref=dst, send_sem=send.at[index], recv_sem=recv.at[index],
            device_id={"grp": me ^ k}, device_id_type=mesh_id,
        )

    def columns(owner):
        return pl.ds(pl.multiple_of(owner * in_cols, in_cols), in_cols)

    def slot(ref, k):
        return ref.at[pl.ds(k * rows, rows), :]

    def result_copy(k):
        return remote(slot(partials, k), results.at[k - 1], k - 1, k)

    def gate_copy(k):
        return remote(gate16.at[:, columns(me ^ k)], gates.at[k], 2 + k, k)

    def rest_copy(k):
        return remote(rest16.at[:, columns(me ^ k)], rests.at[k], 5 + k, k)

    def gated(i, carry):
        base = pl.multiple_of(i * BLOCK, BLOCK)
        here = pl.ds(base, BLOCK)
        scale, pull = norm_parts(sums[:, here])
        x = proj[pl.ds(pl.multiple_of(i * BLOCK + PAD, PAD), BLOCK), :inner].astype(f32)
        sig = sigmoid(x)
        out = y[here, :]
        lit = out * (x * sig)
        grad = dn[here, :].astype(f32)
        gain = wide[1:2]
        normed_out = (lit * scale * gain).astype(bf16).astype(f32)
        d_lit = scale * (grad * gain) - lit * pull
        d_x = (d_lit * out * (sig * (1.0 + x * (1.0 - sig)))).astype(bf16).astype(f32)
        d_gain[0:1, :] += jnp.sum(grad * lit * scale, axis=0, keepdims=True)
        store_rows(moved, base, jnp.concatenate([normed_out, d_x], axis=1), HALF)
        return carry

    lax.fori_loop(0, blocks, gated, 0)
    loads[3].wait()
    loads[4].wait()

    def project(i, carry):
        base = pl.multiple_of(i * BLOCK, BLOCK)
        here = pl.ds(base, BLOCK)
        gather_rows(inverse, base, moved, packed, HALF)
        both = load_rows(packed, 0, BLOCK, 2 * inner // LANES, HALF).astype(bf16)
        left, right = both[:, :inner], both[:, inner:]
        partials[here, :] = nn(left, out16[...]).astype(bf16)
        d_gate[here, :] = right
        out_grad[...] += tn(left, cot[here, :])
        total[:inner, :] += tn(right, normed[here, :])
        for k in range(1, group):

            @pl.when(i == (k + 1) * per - 1)
            def _():
                result_copy(k).start()

        return carry

    lax.fori_loop(0, blocks, project, 0)
    gate16[...] = total[:inner, :].astype(bf16)
    total[...] = jnp.zeros_like(total)
    for k in range(1, group):
        gate_copy(k).start()
    saves = [
        pltpu.make_async_copy(slot(partials, 0), own_result, save.at[0]),
        pltpu.make_async_copy(gate16.at[:, columns(me)], gates.at[0], save.at[1]),
    ]
    for c in saves:
        c.start()
    loads[5].wait()
    loads[6].wait()

    def scan(i, carry):
        backward_block(
            heads, me, blocks - 1 - i, ends, proj, dn, y, states, sums, convw, small, wide, spread, collapse, tri,
            d_conv, d_small, d_skip, moved, after, d_state,
        )
        return carry

    lax.fori_loop(0, blocks, scan, 0)

    def products(i, carry):
        base = pl.multiple_of(i * BLOCK, BLOCK)
        gather_rows(inverse, base, moved, packed, HALF)
        grad = load_rows(packed, 0, BLOCK, channels // LANES + 1, HALF).astype(bf16)
        proj[pl.ds(base, BLOCK), : channels + LANES] = grad
        total[...] += tn(grad, normed[pl.ds(base, BLOCK), :])
        return carry

    lax.fori_loop(0, blocks, products, 0)
    rest16[...] = total[: channels + HEADS, :].astype(bf16)
    for k in range(1, group):
        rest_copy(k).start()
    for k in range(1, group):
        result_copy(k).wait_send()
    for c in saves:
        c.wait()
    saves = [pltpu.make_async_copy(rest16.at[:, columns(me)], rests.at[0], save.at[2])]
    saves[0].start()

    def back(i, carry):
        base = pl.multiple_of(i * BLOCK, BLOCK)
        here = pl.ds(base, BLOCK)
        value = nn(proj[here, :channels], weight[inner:shared, :])
        value = value + nn(proj[here, channels : channels + HEADS], weight[shared:, :])
        value = value + nn(d_gate[here, :], weight[:inner, :])
        partials[here, :] = value.astype(bf16)
        d_norm_gain[0:1, :] += jnp.sum(value * normed[here, :].astype(f32), axis=0, keepdims=True)
        return carry

    lax.fori_loop(0, blocks, back, 0)
    saves += [pltpu.make_async_copy(slot(partials, k), outs[k], save.at[3 + k]) for k in range(group)]
    for c in saves[1:]:
        c.start()
    for k in range(1, group):
        result_copy(k).wait_recv()
        gate_copy(k).wait()
        rest_copy(k).wait()
    for c in saves:
        c.wait()


def back_call(
    heads, rows, ends, inverse, proj, y, states, dn, normed, cot, weight, sums, out16,
    convw, small, wide, spread, collapse, tri,
):
    inner = heads * HEADDIM
    positions, width = proj.shape
    channels = inner + 2 * STATE
    group = positions // rows
    in_cols = D // group
    part = jax.ShapeDtypeStruct((rows, D), bf16)

    def small_out(*shape):
        return jax.ShapeDtypeStruct(shape, f32)

    return pl.pallas_call(
        partial(back_kernel, heads, rows),
        out_shape=[
            part,
            jax.ShapeDtypeStruct((group - 1, rows, D), bf16),
            jax.ShapeDtypeStruct((group, inner, in_cols), bf16),
            jax.ShapeDtypeStruct((group, channels + HEADS, in_cols), bf16),
            part, part, part, part,
            small_out(inner, D), small_out(8, D), small_out(8, inner), small_out(8, channels),
            small_out(8, LANES), small_out(8, inner),
        ],
        in_specs=[SMEM, SMEM] + [ANY] * 7 + [VM] * 8,
        out_specs=[ANY] * 8 + [VM] * 6,
        scratch_shapes=[
            pltpu.VMEM((positions + PAD, width), bf16),
            pltpu.VMEM(y.shape, f32),
            pltpu.VMEM(states.shape, f32),
            pltpu.VMEM(dn.shape, bf16),
            pltpu.VMEM(normed.shape, bf16),
            pltpu.VMEM(cot.shape, bf16),
            pltpu.VMEM(weight.shape, bf16),
            pltpu.VMEM((positions * HALF, LANES), f32),
            pltpu.VMEM((BLOCK * HALF, LANES), f32),
            pltpu.VMEM((positions, D), bf16),
            pltpu.VMEM((positions, inner), bf16),
            pltpu.VMEM((inner, D), bf16),
            pltpu.VMEM((channels + LANES, D), f32),
            pltpu.VMEM((channels + HEADS, D), bf16),
            pltpu.VMEM((8, channels), f32),
            pltpu.VMEM((STATE, inner), f32),
            pltpu.SemaphoreType.DMA((7,)),
            pltpu.SemaphoreType.DMA((7,)),
            pltpu.SemaphoreType.DMA((9,)),
            pltpu.SemaphoreType.DMA((9,)),
        ],
        compiler_params=pltpu.CompilerParams(
            vmem_limit_bytes=60 * 1024 * 1024, collective_id=4, has_side_effects=True
        ),
        name="back",
    )(
        ends, inverse, proj, y, states, dn, normed, cot, weight, sums, out16,
        convw, small, wide, spread, collapse, tri,
    )


def greet(axes, sizes, place):
    total = int(np.prod(sizes))
    barrier = pltpu.get_barrier_semaphore()

    def hail(d, carry):
        pl.semaphore_signal(
            barrier, inc=1, device_id=coordinates(axes, sizes, lax.rem(place + d, total)),
            device_id_type=pl.DeviceIdType.MESH,
        )
        return carry

    lax.fori_loop(1, total, hail, 0)
    pl.semaphore_wait(barrier, total - 1)


def coordinates(axes, sizes, place):
    where = {}
    for axis, size in reversed(list(zip(axes, sizes))):
        where[axis] = lax.rem(place, size)
        place = place // size
    return where


def my_place(axes, sizes):
    place = 0
    for axis, size in zip(axes, sizes):
        place = place * size + lax.axis_index(axis)
    return place


def share_kernel(axes, sizes, x, total, slots, send_sem, recv_sem):
    count = int(np.prod(sizes))
    me = my_place(axes, sizes)
    greet(axes, sizes, me)
    slots[me] = x[...]

    def copy_to(other, slot):
        return pltpu.make_async_remote_copy(
            src_ref=x, dst_ref=slots.at[slot], send_sem=send_sem.at[other], recv_sem=recv_sem.at[slot],
            device_id=coordinates(axes, sizes, other), device_id_type=pl.DeviceIdType.MESH,
        )

    def send(d, carry):
        copy_to(lax.rem(me + d, count), me).start()
        return carry

    def receive(d, carry):
        other = lax.rem(me + d, count)
        copy_to(other, other).wait_recv()
        return carry

    def sent(d, carry):
        copy_to(lax.rem(me + d, count), me).wait_send()
        return carry

    lax.fori_loop(1, count, send, 0)
    lax.fori_loop(1, count, receive, 0)
    lax.fori_loop(1, count, sent, 0)
    total[...] = lax.fori_loop(1, count, lambda i, acc: acc + slots[i], slots[0])


def share_sum(x, axes, sizes, collective_id):
    count = int(np.prod(sizes))
    return pl.pallas_call(
        partial(share_kernel, axes, sizes),
        out_shape=jax.ShapeDtypeStruct(x.shape, f32),
        in_specs=[pl.BlockSpec(memory_space=pltpu.VMEM)],
        out_specs=pl.BlockSpec(memory_space=pltpu.VMEM),
        scratch_shapes=[
            pltpu.VMEM((count,) + x.shape, f32),
            pltpu.SemaphoreType.DMA((count,)),
            pltpu.SemaphoreType.DMA((count,)),
        ],
        compiler_params=pltpu.CompilerParams(collective_id=collective_id, has_side_effects=True),
        name="share_sum",
    )(x)


def reduce_kernel(axes, sizes, x, total, slots, mine, send_sem, recv_sem, send_back, recv_back):
    count = int(np.prod(sizes))
    me = my_place(axes, sizes)
    greet(axes, sizes, me)
    slots[me] = x[me]

    def copy_to(other, slot):
        return pltpu.make_async_remote_copy(
            src_ref=x.at[other], dst_ref=slots.at[slot],
            send_sem=send_sem.at[other], recv_sem=recv_sem.at[slot],
            device_id=coordinates(axes, sizes, other), device_id_type=pl.DeviceIdType.MESH,
        )

    def copy_back(other, slot):
        return pltpu.make_async_remote_copy(
            src_ref=mine, dst_ref=total.at[slot],
            send_sem=send_back.at[other], recv_sem=recv_back.at[slot],
            device_id=coordinates(axes, sizes, other), device_id_type=pl.DeviceIdType.MESH,
        )

    def each(action):
        def one(d, carry):
            action(lax.rem(me + d, count))
            return carry

        lax.fori_loop(1, count, one, 0)

    each(lambda other: copy_to(other, me).start())
    each(lambda other: copy_to(other, other).wait_recv())
    mine[...] = lax.fori_loop(1, count, lambda i, acc: acc + slots[i], slots[0])
    total[me] = mine[...]
    each(lambda other: copy_back(other, me).start())
    each(lambda other: copy_to(other, me).wait_send())
    each(lambda other: copy_back(other, other).wait_recv())
    each(lambda other: copy_back(other, me).wait_send())


def reduce_sum(x, axes, sizes, collective_id):
    count = int(np.prod(sizes))
    return pl.pallas_call(
        partial(reduce_kernel, axes, sizes),
        out_shape=jax.ShapeDtypeStruct(x.shape, f32),
        in_specs=[pl.BlockSpec(memory_space=pltpu.VMEM)],
        out_specs=pl.BlockSpec(memory_space=pltpu.VMEM),
        scratch_shapes=[
            pltpu.VMEM(x.shape, f32),
            pltpu.VMEM(x.shape[1:], f32),
            pltpu.SemaphoreType.DMA((count,)),
            pltpu.SemaphoreType.DMA((count,)),
            pltpu.SemaphoreType.DMA((count,)),
            pltpu.SemaphoreType.DMA((count,)),
        ],
        compiler_params=pltpu.CompilerParams(collective_id=collective_id, has_side_effects=True),
        name="reduce_sum",
    )(x)


def assemble_kernel(group, heads, me, error, factor, gates, rests, grad, merged, left):
    inner = heads * HEADDIM
    turn = pl.program_id(0)
    exact_rows = 2 * STATE + HEADS

    for k in range(group):
        for piece, part in ((0, gates), (1, rests)):

            @pl.when(turn == piece * group + (me[0] ^ k))
            def _():
                grad[...] = part[k, :inner, :].astype(f32)

    @pl.when(turn == 2 * group)
    def _():
        total = rests[0, inner:, :].astype(f32)
        for k in range(1, group):
            total = total + rests[k, inner:, :].astype(f32)
        grad[:exact_rows, :] = total
        grad[exact_rows:, :] = jnp.zeros((inner - exact_rows, grad.shape[1]), f32)

    sides = lax.broadcasted_iota(jnp.int32, (inner, 1), 0)
    known = sides < jnp.where(turn == 2 * group, exact_rows, inner)
    total = jnp.where(known, grad[...] + error[...], 0.0)
    merged[...] = total
    lanes = lax.broadcasted_iota(jnp.int32, factor.shape, 1)
    rows = jnp.where(lanes < jnp.where(turn == 2 * group, exact_rows, inner), factor[...], 0.0)
    part = lax.dot_general(
        rows, total, (((1,), (0,)), ((), ())), precision=highest, preferred_element_type=f32
    )
    left[...] = jnp.where(turn == 0, part, left[...] + part)


def assemble(heads, me, error, factor, gates, rests):
    group = gates.shape[0]
    inner = heads * HEADDIM
    rows, columns = error.shape
    tall = pl.BlockSpec((inner, columns), lambda i: (i, 0))
    return pl.pallas_call(
        partial(assemble_kernel, group, heads),
        grid=(2 * group + 1,),
        out_shape=[jax.ShapeDtypeStruct((rows, columns), f32)] * 2
        + [jax.ShapeDtypeStruct((factor.shape[0], columns), f32)],
        in_specs=[SMEM, tall, pl.BlockSpec((factor.shape[0], inner), lambda i: (0, i))]
        + [whole(gates), whole(rests)],
        out_specs=[tall] * 2 + [pl.BlockSpec((factor.shape[0], columns), lambda i: (0, 0))],
        compiler_params=pltpu.CompilerParams(vmem_limit_bytes=VMEM_LIMIT),
        name="assemble",
    )(me, error, factor, gates, rests)


def update_kernel(tall, flat, merged, moment, master, master_new, moment_new, error_new):
    approx = lax.dot_general(
        tall[...], flat[...], (((0,), (0,)), ((), ())), precision=highest, preferred_element_type=f32
    )
    fresh = momentum_decay * moment[...] + approx
    moment_new[...] = fresh
    master_new[...] = master[...] - weight_rate * fresh
    error_new[...] = merged[...] - approx


def update(tall, flat, merged, moment, master, step):
    rows, columns = merged.shape
    block = pl.BlockSpec((step, columns), lambda i: (i, 0))
    return pl.pallas_call(
        update_kernel,
        grid=(pl.cdiv(rows, step),),
        out_shape=[jax.ShapeDtypeStruct((rows, columns), f32)] * 3,
        in_specs=[pl.BlockSpec((tall.shape[0], step), lambda i: (0, i)), whole(flat)] + [block] * 3,
        out_specs=[block] * 3,
        compiler_params=pltpu.CompilerParams(vmem_limit_bytes=VMEM_LIMIT),
        name="update",
    )(tall, flat, merged, moment, master)


def split_vectors(vectors):
    widths = [D, CONV * XBC, XBC, HEADS, HEADS, HEADS, INNER]
    pieces = []
    offset = 0
    for span_size in widths:
        pieces.append(vectors[offset : offset + span_size])
        offset = offset + span_size
    norm_gain, conv_flat, conv_bias, dt_bias, decay_log, skip_gain, gate_gain = pieces
    return (
        norm_gain,
        conv_flat.reshape(CONV, XBC),
        conv_bias,
        dt_bias,
        decay_log,
        skip_gain,
        gate_gain,
    )


def spread_of(heads):
    lanes = np.arange(LANES)[:, None]
    return np.where(
        (lanes < 3 * heads) & (lanes % heads == np.arange(heads * HEADDIM)[None] // HEADDIM), 1.0, 0.0
    )


def collapse_of(heads):
    return np.where(np.arange(heads * HEADDIM)[:, None] // HEADDIM == np.arange(LANES)[None], 1.0, 0.0)


def local(
    tokens,
    cotangent,
    order,
    lengths,
    vectors,
    vector_moment,
    in_master,
    in_moment,
    in_error,
    in_factor,
    out_master,
    out_moment,
    out_error,
    out_factor,
):
    replicas = lax.axis_size("rep")
    group = lax.axis_size("grp")
    me = lax.axis_index("grp")
    heads = HEADS // group
    inner = INNER // group
    keys = 2 * STATE

    norm_gain, conv_weight, conv_bias, dt_bias, decay_log, skip_gain, gate_gain = split_vectors(vectors)

    def swap(x, k):
        return lax.ppermute(x, "grp", [(i, i ^ k) for i in range(group)])

    in_master, in_moment, in_error = in_master.T, in_moment.T, in_error[0].T
    in_factor, out_factor = in_factor.T, out_factor.T
    in_cols = in_master.shape[1]

    in16 = in_master.astype(bf16)

    stream = tokens[0].astype(f32)
    inv_rms = lax.rsqrt(jnp.mean(stream * stream, axis=-1, keepdims=True) + epsilon)
    normed_own = (stream * inv_rms * norm_gain).astype(bf16)
    normed_parts = [normed_own] + [swap(normed_own, k) for k in range(1, group)]
    normed = jnp.concatenate(normed_parts, axis=0)
    cot_own, normed = lax.optimization_barrier((cotangent[0], normed))
    cot_all = jnp.concatenate([cot_own] + [swap(cot_own, k) for k in range(1, group)], axis=0)
    positions = order.shape[1]
    rows = positions // group
    slots = ((order // rows) ^ me) * rows + order % rows
    place = jnp.reshape(me, (1,)).astype(jnp.int32)
    packed = lax.broadcasted_iota(jnp.int32, (positions, 1), 0)
    inverse = jnp.sum(jnp.where(slots.T == packed.T, packed, 0), axis=0, keepdims=True)

    ends = jnp.cumsum(lengths[0]).astype(jnp.int32)

    def own(a, size):
        return lax.dynamic_slice_in_dim(a, me * size, size, axis=a.ndim - 1)

    conv_all = jnp.concatenate([conv_weight, conv_bias[None]], axis=0)
    convw = jnp.concatenate([own(conv_all[:, :INNER], inner), conv_all[:, INNER:]], axis=1)
    convw = jnp.pad(convw, ((0, 8 - CONV - 1), (0, 0)))
    small = jnp.stack([own(dt_bias, heads), own(jnp.exp(decay_log), heads)])
    small = jnp.pad(small, ((0, 6), (0, LANES - heads)))
    own_gain = own(gate_gain, inner)
    wide = jnp.stack([jnp.repeat(own(skip_gain, heads), HEADDIM), own_gain])
    wide = jnp.pad(wide, ((0, 6), (0, 0)))
    spread = jnp.asarray(spread_of(heads), bf16)
    collapse = jnp.asarray(collapse_of(heads), bf16)
    tri = jnp.asarray(np.tril(np.ones((BLOCK, BLOCK))), bf16)

    out16 = out_master.astype(bf16)
    weight, normed, cot_all, proj, y, states, dn, sums = front_call(
        heads, ends, slots, normed_own, cotangent[0], in16, out16, convw, small, wide, spread, tri
    )
    sums8 = jnp.pad(jnp.stack([sums[0], sums[8]]), ((0, 6), (0, 0)))
    (
        own_result, results, gates, rests, back0, back1, back2, back3,
        out_owned, d_norm_gain, d_gain, d_conv, d_small, d_skip,
    ) = back_call(
        heads, rows, ends, inverse, proj, y, states, dn, normed, cot_all, weight, sums8, out16,
        convw, small, wide, spread, collapse, tri,
    )
    d_normed = back0.astype(f32)
    for k, part in enumerate((back1, back2, back3)):
        d_normed = d_normed + swap(part, k + 1).astype(f32)
    result = stream + own_result.astype(f32)
    for k in range(group - 1):
        result = result + results[k].astype(f32)
    mixed_rows = result.astype(bf16)[None]
    in_owned, in_merged, in_left = assemble(heads, place, in_error, in_factor, gates, rests)
    d_norm_gain = d_norm_gain[0] / norm_gain
    scaled = d_normed * norm_gain
    lean = jnp.mean(scaled * stream, axis=-1, keepdims=True)
    d_stream = inv_rms * scaled - stream * (inv_rms * inv_rms * inv_rms * lean)
    input_rows = (cotangent[0].astype(f32) + d_stream).astype(bf16)[None]

    def placed(a, total):
        size = a.shape[-1]
        zero = jnp.zeros(a.shape[:-1] + (total,), f32)
        return lax.dynamic_update_slice_in_dim(zero, a, me * size, axis=a.ndim - 1)

    d_conv_all = jnp.concatenate([placed(d_conv[:5, :inner], INNER), d_conv[:5, inner:]], axis=1)
    d_skip = jnp.sum(d_skip[0].reshape(heads, HEADDIM), axis=1)
    vector_local = jnp.concatenate(
        [
            d_norm_gain,
            d_conv_all[:CONV].reshape(-1),
            d_conv_all[CONV],
            placed(d_small[0, :heads], HEADS),
            placed(d_small[1, :heads], HEADS),
            placed(d_skip, HEADS),
            placed(d_gain[0], INNER),
        ]
    )

    out_merged = out_owned + out_error[0]

    def exact(a, b, dims):
        return lax.dot_general(a, b, (dims, ((), ())), precision=highest, preferred_element_type=f32)

    left = jnp.concatenate([in_left, exact(out_factor, out_merged, ((1,), (1,)))], axis=1)
    left = share_sum(left, ("rep",), (replicas,), 1)
    in_left, out_left = left[:, :in_cols], left[:, in_cols:]
    rank = left.shape[0]
    grams = jnp.concatenate([exact(in_left, in_left, ((1,), (1,))), exact(out_left, out_left, ((1,), (1,)))], axis=1)
    bundle = [
        exact(in_left, in_merged, ((1,), (1,))),
        exact(out_left, out_merged, ((1,), (0,))),
        grams,
        jnp.pad(vector_local, (0, -vector_local.size % rank)).reshape(rank, -1),
    ]
    bundle = [jnp.pad(b, ((0, 0), (0, -b.shape[1] % LANES))) for b in bundle]
    edges = np.cumsum([0] + [b.shape[1] for b in bundle])
    devices = group * replicas
    share = -(-int(edges[-1]) // (devices * LANES)) * LANES
    packed = jnp.pad(jnp.concatenate(bundle, axis=1), ((0, 0), (0, devices * share - int(edges[-1]))))
    packed = jnp.swapaxes(packed.reshape(rank, devices, share), 0, 1)
    packed = reduce_sum(packed, ("grp", "rep"), (group, replicas), 2)
    packed = jnp.swapaxes(packed, 0, 1).reshape(rank, devices * share)
    in_right, out_right, grams, vector_sum = [
        packed[:, edges[i] : edges[i + 1]] for i in range(4)
    ]
    columns = -(-vectors.shape[0] // rank)
    vector_grad = vector_sum[:, :columns].reshape(-1)[: vectors.shape[0]] / replicas

    def settle(gram, left_t, right_t):
        inverse = lax.linalg.triangular_solve(
            jnp.linalg.cholesky(gram / replicas), jnp.eye(rank, dtype=f32), left_side=True, lower=True
        )
        return exact(inverse, left_t, ((1,), (0,))), exact(inverse, right_t, ((1,), (0,))) / replicas

    in_basis, in_right = settle(grams[:, :rank], in_left, in_right[:, : in_master.shape[0]])
    out_basis, out_right = settle(grams[:, rank : 2 * rank], out_left, out_right[:, : out_master.shape[1]])
    in_new, in_moment_new, in_error_new = update(
        in_right, in_basis, in_merged, in_moment, in_master, inner
    )
    out_new, out_moment_new, out_error_new = update(
        out_basis, out_right, out_merged, out_moment, out_master, LANES
    )
    vector_moment_new = momentum_decay * vector_moment + vector_grad
    vector_new = vectors - vector_rate * vector_moment_new
    return (
        mixed_rows,
        input_rows,
        in_owned.T[None],
        out_owned[None],
        vector_grad,
        in_new.T,
        in_moment_new.T,
        in_error_new.T[None],
        in_right.T,
        out_new,
        out_moment_new,
        out_error_new[None],
        out_right.T,
        vector_new,
        vector_moment_new,
    )


def solution(mesh):
    placed = (
        P("rep", "grp", None),
        P("rep", "grp", None),
        P("rep", None),
        P("rep", None),
        P(),
        P(),
        P("grp", None),
        P("grp", None),
        P("rep", "grp", None),
        P(),
        P("grp", None),
        P("grp", None),
        P("rep", "grp", None),
        P(),
    )
    return jax.shard_map(
        local,
        mesh=mesh,
        in_specs=placed,
        out_specs=(
            P("rep", "grp", None),
            P("rep", "grp", None),
            P("rep", "grp", None),
            P("rep", "grp", None),
            P(),
            P("grp", None),
            P("grp", None),
            P("rep", "grp", None),
            P(),
            P("grp", None),
            P("grp", None),
            P("rep", "grp", None),
            P(),
            P(),
            P(),
        ),
        check_vma=False,
    )
```
